128 devices in a mesh: dom: 4 (over x), dev: 32 (over y, z, core).
Axes of the slice: x: 4, y: 4, z: 4, core: 2. Of those that a mesh axis runs over, the one named last changes fastest.
Arguments:
- node_query: bfloat16 [131072, 256], P(('dom', 'dev')), may hold values from -112 to 112
- node_key: bfloat16 [131072, 256], P(('dom', 'dev')), may hold values from -4 to 4
- node_value: bfloat16 [131072, 256], P(('dom', 'dev')), may hold values from -6 to 6
- cotangent: bfloat16 [131072, 256], P(('dom', 'dev')), may hold values from -6 to 6
- virtual_key: bfloat16 [512, 256], P(('dom', 'dev')), may hold values from -6 to 6
- virtual_value: bfloat16 [512, 256], P(('dom', 'dev')), may hold values from -6 to 6
- local_blocks: int32 [1024, 16], P(('dom', 'dev')), may hold values from 0 to 1023, as said below
- expander_dev: int32 [1024, 4], P(('dom', 'dev')), may hold values from 0 to 31, all different within a row; in each aligned block of 8 rows (0 to 7, 8 to 15, ...) at most 2 rows name the same one
- expander_pos: int32 [1024, 4], P(('dom', 'dev')), may hold values from 0 to 7
- far_group: int32 [1024, 4], P(('dom', 'dev')), may hold values from 1 to 3
- far_pos: int32 [1024, 4], P(('dom', 'dev')), may hold values from 0 to 7
Outputs:
- attended: bfloat16 [131072, 256], P(('dom', 'dev'))
- query_grad: float32 [131072, 256], P(('dom', 'dev'))
- key_grad: float32 [131072, 256], P(('dom', 'dev'))
- value_grad: float32 [131072, 256], P(('dom', 'dev'))
- virtual_key_grad: float32 [512, 256], P(('dom', 'dev'))
- virtual_value_grad: float32 [512, 256], P(('dom', 'dev'))
The draws below stay inside these ranges and needn't reach their ends.
Inputs may be any that keep to these rules, and one draw needn't show every extreme that they name: `local_blocks`: row b names distinct blocks of b's own group, each at a cyclic distance of at most 8 from b inside the group; the first entry is b itself. `expander_dev`: A row names distinct devices; in the rows of one device (aligned blocks of 8 rows) no device is named more than 2 times.
All inputs are finite; a program needn't handle non-finite values.
Results may differ from the reference program's by a relative error of at most 0.04.
Values may be sent and summed in bfloat16 or wider, within the bound.
A program may use at most 256 MiB of HBM per device.

```python
import math
import jax
import jax.numpy as jnp
import numpy as np
from jax import lax

BLK = 128
NB = 8
H = 4
HB = 8
LOC = 16
XG = 4
XF = 4
VB = 128
HEAD_FEATURES = 256
CAP = 2
BLOCKS = 1024
NODE_TOTAL = 131072
VIRTUAL_NODES = 512
N_DOM = 4
N_DEV = 32


def shared_base(key):
    return jnp.clip(jax.random.normal(key, (NODE_TOTAL, HEAD_FEATURES), jnp.float32), -4.0, 4.0)


def draw_node_key(key, part):
    common = shared_base(key)
    drawn = common
    return drawn.astype(jnp.bfloat16)


def draw_node_query(key, part):
    key = jax.random.fold_in(key, 9)
    drawn = 2.0 * jnp.clip(jax.random.normal(key, (NODE_TOTAL, HEAD_FEATURES), jnp.float32), -4.0, 4.0)
    return drawn.astype(jnp.bfloat16)


def pick_offsets(row_key):
    return jax.random.permutation(row_key, 2 * HB)[:LOC - 1]


def draw_local_blocks(key, part):
    key = jax.random.fold_in(key, 5)
    row_keys = jax.random.split(key, BLOCKS)
    chosen = jax.vmap(pick_offsets)(row_keys).astype(jnp.int32)
    offsets = jnp.where(chosen < HB, chosen - HB, chosen - HB + 1)
    offsets = jnp.concatenate([jnp.zeros((BLOCKS, 1), jnp.int32), offsets], axis=1)
    block_ids = jnp.arange(BLOCKS, dtype=jnp.int32)[:, None]
    group_blocks = NB * N_DEV
    anchor = block_ids // group_blocks * group_blocks
    return (anchor + (block_ids % group_blocks + offsets) % group_blocks).astype(jnp.int32)


def place_ends(entries, rng, low, top_value):
    place = [jax.random.randint(jax.random.fold_in(rng, axis), (), 0, length) for axis, length in enumerate(entries.shape)]
    longest = entries.shape.index(max(entries.shape))
    neighbour = place[:longest] + [(place[longest] + 1) % entries.shape[longest]] + place[longest + 1:]
    return entries.at[tuple(place)].set(low).at[tuple(neighbour)].set(top_value)


def block_levels(key, extent, shards, least, top_value):
    factor_of = 1.0
    for dim, blocks in shards:
        heights = jax.random.uniform(jax.random.fold_in(jax.random.fold_in(key, 6), dim), (blocks,), jnp.float32, least / len(shards), top_value / len(shards))
        factor_of = factor_of * jnp.repeat(jnp.exp(heights), extent[dim] // blocks).reshape((-1,) + (1,) * (len(extent) - 1 - dim))
    return factor_of


def assign_block(stream_key, own, number, rows, amount, top, bound, slope):
    order = jax.random.permutation(stream_key, amount)
    heavy_load, usual = portions_of(amount, rows * top, bound, slope, True), portions_of(amount, rows * top, bound, slope, False)
    places = jnp.arange(amount)

    def named(lengths, turn):
        used = int((lengths > 0).sum())
        fixed = max(1, used // 4)
        moved = fixed + (places - fixed + turn * (used - fixed)) % max(1, amount - fixed)
        return jnp.zeros((amount,), jnp.int32).at[order[jnp.where(places < fixed, places, moved)]].set(jnp.asarray(lengths, jnp.int32))

    lengths = jnp.where(number % 4 == 0, named(heavy_load, number // 4), named(usual, number - number // 4 - 1))
    mixed = jax.random.permutation(jax.random.fold_in(own, 3), amount)
    donor, taker = mixed[0:amount // 2 * 2:2], mixed[1:amount // 2 * 2:2]
    room = jnp.minimum(lengths[donor] - 1, bound - lengths[taker]) // 2
    room = jnp.where((donor == order[0]) | (taker == order[0]) | (lengths[taker] == 0), 0, jnp.maximum(room, 0))
    moved = jax.random.randint(jax.random.fold_in(own, 4), (amount // 2,), 0, 1 << 20) % (room + 1)
    lengths = lengths.at[donor].add(-moved).at[taker].add(moved)
    items = jnp.searchsorted(jnp.cumsum(lengths), jnp.arange(rows * top), side="right").astype(jnp.int32)
    grid = items.reshape(top, rows).T
    grid = grid[jax.random.permutation(jax.random.fold_in(own, 1), rows)]
    turn = jax.random.randint(jax.random.fold_in(own, 2), (rows, 1), 0, top)
    return jnp.take_along_axis(grid, (jnp.arange(top)[None, :] + turn) % top, axis=1)


def portions_of(number_of, total, bound, lean, full):
    weights = [(1 << 20) // math.isqrt(rank ** lean) + 1 for rank in range(1, number_of + 1)]
    largest = bound if full else min(bound, max(-(-total // number_of), total * weights[0] // sum(weights)))
    least = 1 if total - largest >= number_of - 1 else 0
    given, rest = [largest] + [least] * (number_of - 1), total - largest - least * (number_of - 1)
    while rest > 0:
        movable = [i for i in range(1, number_of) if given[i] < largest] or [i for i in range(1, number_of) if given[i] < bound]
        whole, remaining = sum([weights[i] for i in movable]), rest
        for i in movable:
            more = min(bound - given[i], max(1, remaining * weights[i] // whole), rest)
            given[i] = given[i] + more
            rest = rest - more
    return np.array(given)


def centred(own_key, shape, scale, reach, shards=(), held_as=jnp.bfloat16):
    loudness = block_levels(own_key, shape, shards, -0.22, 0.18) if shards else 1.0
    entries = jax.random.normal(own_key, shape, jnp.float32) * scale * loudness
    return jnp.minimum(jnp.maximum(entries, -reach), reach).astype(held_as)


def setup_inputs(seed: int = 0) -> dict:
    splits = jax.random.split(jax.random.key(seed), 12)
    node_query = draw_node_query(jax.random.fold_in(splits[11], 71), 0)
    node_key = draw_node_key(jax.random.fold_in(splits[11], 71), 0)
    node_value = centred(splits[2], (NODE_TOTAL, HEAD_FEATURES), 1.0, 6.0, ((0, 128),))
    cotangent = centred(splits[3], (NODE_TOTAL, HEAD_FEATURES), 1.0, 6.0, ((0, 128),))
    virtual_key = centred(splits[4], (VIRTUAL_NODES, HEAD_FEATURES), 1.0, 6.0, ((0, 128),))
    virtual_value = centred(splits[5], (VIRTUAL_NODES, HEAD_FEATURES), 1.0, 6.0, ((0, 128),))
    local_blocks = draw_local_blocks(jax.random.fold_in(splits[11], 71), 0)
    expander_dev_keys = jax.random.split(jax.random.fold_in(splits[7], 1), BLOCKS // NB)
    expander_dev_turns = jax.random.permutation(jax.random.fold_in(splits[7], 3), BLOCKS // NB)
    expander_dev = jax.vmap(lambda own, number: assign_block(jax.random.fold_in(splits[7], 2), own, number, NB, N_DEV, XG, CAP, 2))(expander_dev_keys, expander_dev_turns).reshape((BLOCKS, XG))
    expander_pos = place_ends(jax.random.randint(splits[8], (BLOCKS, XG), 0, NB), jax.random.fold_in(splits[8], 1), 0, NB - 1).astype(jnp.int32)
    far_group = place_ends(jax.random.randint(splits[9], (BLOCKS, XF), 1, N_DOM), jax.random.fold_in(splits[9], 1), 1, N_DOM - 1).astype(jnp.int32)
    far_pos = place_ends(jax.random.randint(splits[10], (BLOCKS, XF), 0, NB), jax.random.fold_in(splits[10], 1), 0, NB - 1).astype(jnp.int32)
    return {"node_query": node_query, "node_key": node_key, "node_value": node_value, "cotangent": cotangent, "virtual_key": virtual_key, "virtual_value": virtual_value, "local_blocks": local_blocks, "expander_dev": expander_dev, "expander_pos": expander_pos, "far_group": far_group, "far_pos": far_pos}


def attend_block(query_rows, grad_rows, key_rows, value_rows):
    row_count, feature_width = query_rows.shape
    head_size = feature_width // H
    score_scale = head_size ** -0.5
    query_heads = query_rows.astype(jnp.float32).reshape(row_count, H, head_size)
    grad_heads = grad_rows.astype(jnp.float32).reshape(row_count, H, head_size)
    key_heads = key_rows.astype(jnp.float32).reshape(-1, H, head_size)
    value_heads = value_rows.astype(jnp.float32).reshape(-1, H, head_size)
    scores = jnp.einsum("ihd,jhd->hij", query_heads, key_heads) * score_scale
    row_max = jnp.max(scores, axis=2, keepdims=True)
    log_total = row_max + jnp.log(jnp.sum(jnp.exp(scores - row_max), axis=2, keepdims=True))
    weights = jnp.exp(scores - log_total)
    weights_low = lax.optimization_barrier(weights.astype(jnp.bfloat16)).astype(jnp.float32)
    target_block = jnp.einsum("hij,jhd->ihd", weights_low, value_heads)
    target_block = target_block.reshape(row_count, feature_width).astype(jnp.bfloat16)
    row_dot = jnp.sum((grad_rows.astype(jnp.float32) * target_block.astype(jnp.float32)).reshape(row_count, H, head_size), axis=2).T
    grad_weights = jnp.einsum("ihd,jhd->hij", grad_heads, value_heads)
    grad_scores = weights * (grad_weights - row_dot[:, :, None])
    grad_scores = lax.optimization_barrier(grad_scores.astype(jnp.bfloat16)).astype(jnp.float32)
    query_contribution = jnp.einsum("hij,jhd->ihd", grad_scores, key_heads).reshape(row_count, feature_width) * score_scale
    value_terms = jnp.einsum("hij,ihd->jhd", weights_low, grad_heads).reshape(-1, feature_width).astype(jnp.bfloat16)
    key_contributions = (jnp.einsum("hij,ihd->jhd", grad_scores, query_heads) * score_scale).reshape(-1, feature_width).astype(jnp.bfloat16)
    return target_block, query_contribution, key_contributions, value_terms


def reference(node_query, node_key, node_value, cotangent, virtual_key, virtual_value, local_blocks, expander_dev, expander_pos, far_group, far_pos):
    group_blocks = NB * N_DEV
    query_blocks = node_query.reshape(BLOCKS, BLK, HEAD_FEATURES)
    grad_blocks = cotangent.reshape(BLOCKS, BLK, HEAD_FEATURES)
    key_blocks = node_key.reshape(BLOCKS, BLK, HEAD_FEATURES)
    value_blocks = node_value.reshape(BLOCKS, BLK, HEAD_FEATURES)
    block_ids = jnp.arange(BLOCKS, dtype=jnp.int32)
    group_of = block_ids // group_blocks
    member = (block_ids // NB) % N_DEV
    group_ids = (group_of[:, None] * N_DEV + expander_dev) * NB + expander_pos
    far_ids = (((group_of[:, None] + far_group) % N_DOM) * N_DEV + member[:, None]) * NB + far_pos
    key_lists = jnp.concatenate([local_blocks, group_ids, far_ids], axis=1).astype(jnp.int32)
    listed = key_lists.shape[1]
    divided_rows = listed * BLK
    virtual_keys = virtual_key.reshape(N_DOM, VB, HEAD_FEATURES)
    virtual_values = virtual_value.reshape(N_DOM, VB, HEAD_FEATURES)

    def step(carried_totals, block_index):
        key_accumulator, value_accumulator, virtual_key_accumulator, virtual_value_accumulator = carried_totals
        chosen = key_lists[block_index]
        resident_group = block_index // group_blocks
        key_rows = jnp.concatenate([key_blocks[chosen].reshape(-1, HEAD_FEATURES), virtual_keys[resident_group]], axis=0)
        value_rows = jnp.concatenate([value_blocks[chosen].reshape(-1, HEAD_FEATURES), virtual_values[resident_group]], axis=0)
        target_block, query_contribution, key_contributions, value_terms = attend_block(query_blocks[block_index], grad_blocks[block_index], key_rows, value_rows)
        key_accumulator = key_accumulator.at[chosen].add(key_contributions[:divided_rows].astype(jnp.float32).reshape(listed, BLK, HEAD_FEATURES))
        value_accumulator = value_accumulator.at[chosen].add(value_terms[:divided_rows].astype(jnp.float32).reshape(listed, BLK, HEAD_FEATURES))
        virtual_key_accumulator = virtual_key_accumulator.at[resident_group].add(key_contributions[divided_rows:].astype(jnp.float32))
        virtual_value_accumulator = virtual_value_accumulator.at[resident_group].add(value_terms[divided_rows:].astype(jnp.float32))
        return (key_accumulator, value_accumulator, virtual_key_accumulator, virtual_value_accumulator), (target_block, query_contribution)

    start = (jnp.zeros((BLOCKS, BLK, HEAD_FEATURES), jnp.float32), jnp.zeros((BLOCKS, BLK, HEAD_FEATURES), jnp.float32),
             jnp.zeros((N_DOM, VB, HEAD_FEATURES), jnp.float32), jnp.zeros((N_DOM, VB, HEAD_FEATURES), jnp.float32))
    carried_totals, outputs = lax.scan(step, start, block_ids)
    key_accumulator, value_accumulator, virtual_key_accumulator, virtual_value_accumulator = carried_totals
    attended, query_grad = outputs
    return (attended.reshape(NODE_TOTAL, HEAD_FEATURES), query_grad.reshape(NODE_TOTAL, HEAD_FEATURES), key_accumulator.reshape(NODE_TOTAL, HEAD_FEATURES),
            value_accumulator.reshape(NODE_TOTAL, HEAD_FEATURES), virtual_key_accumulator.reshape(VIRTUAL_NODES, HEAD_FEATURES), virtual_value_accumulator.reshape(VIRTUAL_NODES, HEAD_FEATURES))
```

```python
import functools

import jax
import jax.numpy as jnp
from jax import lax
from jax.experimental import pallas as pl
from jax.experimental.pallas import tpu as pltpu
from jax.sharding import PartitionSpec as P

HB = 8
XG = 4
XF = 4
LOC = 16
BLK = 128
HEAD = 64
FEAT = 256
HALF = 128
PAIR = 2 * BLK
VMEM_LIMIT = 56 * 1024 * 1024


def shifted(value, axis, steps):
    count = lax.axis_size(axis)
    return lax.ppermute(value, axis, [(i, (i + steps) % count) for i in range(count)])


def dot(a, b):
    return jnp.dot(a, b, preferred_element_type=jnp.float32)


def flip(tile):
    return tile.astype(jnp.float32).T.astype(tile.dtype)


def heads_on_lanes(tile_t):
    row = lax.broadcasted_iota(jnp.int32, tile_t.shape, 0)
    zero = jnp.zeros_like(tile_t)
    return jnp.concatenate(
        [jnp.where(row < HEAD, tile_t, zero), jnp.where(row >= HEAD, tile_t, zero)], axis=1
    )


def heads_on_rows(tile):
    column = lax.broadcasted_iota(jnp.int32, tile.shape, 1)
    zero = jnp.zeros_like(tile)
    return jnp.concatenate(
        [jnp.where(column < HEAD, tile, zero), jnp.where(column >= HEAD, tile, zero)], axis=0
    )


def own_head(wide):
    return jnp.concatenate([wide[:HEAD, :BLK], wide[HEAD:, BLK:]], axis=0)


def virtual_pick(count, virtual_rows, pad_rows, part):
    shape = (count * virtual_rows, count * pad_rows)
    node = lax.broadcasted_iota(jnp.int32, shape, 0)
    place = lax.broadcasted_iota(jnp.int32, shape, 1)
    wanted = node // virtual_rows * pad_rows + part * virtual_rows + node % virtual_rows
    return (wanted == place).astype(jnp.bfloat16)


def reply_kernel(capacity, wanted_ref, kv_ref, virtual_ref, pay_ref, tail, sems, tail_sem):
    count = pay_ref.shape[0]
    tail[...] = jnp.broadcast_to(virtual_ref[...][None], tail.shape)
    tail_copy = pltpu.make_async_copy(
        tail, pay_ref.at[:, pl.ds(capacity * PAIR, tail.shape[1]), :], tail_sem
    )
    tail_copy.start()
    copies = []
    for device in range(count):
        for slot in range(capacity):
            position = jnp.clip(wanted_ref[device, slot] - 1, 0, kv_ref.shape[0] - 1)
            copies.append(
                pltpu.make_async_copy(
                    kv_ref.at[position],
                    pay_ref.at[device, pl.ds(slot * PAIR, PAIR), :],
                    sems.at[device * capacity + slot],
                )
            )
            copies[-1].start()
    for copy in copies:
        copy.wait()
    tail_copy.wait()


def make_reply(wanted, kv, virtual_rows, capacity):
    count = wanted.shape[0]
    rows = virtual_rows.shape[0]
    return pl.pallas_call(
        functools.partial(reply_kernel, capacity),
        out_shape=jax.ShapeDtypeStruct((count, capacity * PAIR + rows, HALF), jnp.bfloat16),
        in_specs=[
            pl.BlockSpec(memory_space=pltpu.SMEM),
            pl.BlockSpec(memory_space=pltpu.VMEM),
            pl.BlockSpec(memory_space=pltpu.VMEM),
        ],
        out_specs=pl.BlockSpec(memory_space=pl.ANY),
        scratch_shapes=[
            pltpu.VMEM((count, rows, HALF), jnp.bfloat16),
            pltpu.SemaphoreType.DMA((count * capacity,)),
            pltpu.SemaphoreType.DMA,
        ],
        compiler_params=pltpu.CompilerParams(vmem_limit_bytes=VMEM_LIMIT),
    )(wanted, kv, virtual_rows)


def attend_kernel(
    sizes,
    chosen_ref,
    query_ref,
    grad_ref,
    own_ref,
    below_ref,
    above_ref,
    far_refs,
    pay_ref,
    target_ref,
    query_grad_ref,
    own_out,
    below_out,
    above_out,
    far_outs,
    pay_out,
    table,
    flipped,
    tail,
    total,
    scratch,
    sems,
):
    own_blocks, far_count, count, capacity, virtual_rows, pad_rows = sizes
    far_start = own_blocks + 2 * HB
    virtual_at = far_start + far_count * own_blocks
    slots_at = virtual_at + 1
    step = pl.program_id(0)

    @pl.when(step == 0)
    def _():
        moves = [
            (below_ref, table.at[pl.ds(0, HB)]),
            (own_ref, table.at[pl.ds(HB, own_blocks)]),
            (above_ref, table.at[pl.ds(HB + own_blocks, HB)]),
        ]
        for k, far_ref in enumerate(far_refs):
            moves.append((far_ref, table.at[pl.ds(far_start + k * own_blocks, own_blocks)]))
        for slot in range(capacity):
            moves.append(
                (
                    pay_ref.at[:, pl.ds(slot * PAIR, PAIR), :],
                    table.at[pl.ds(slots_at + slot * count, count)],
                )
            )
        moves.append((pay_ref.at[:, pl.ds(capacity * PAIR, pad_rows), :], tail))
        copies = [
            pltpu.make_async_copy(source, target, sems.at[i])
            for i, (source, target) in enumerate(moves)
        ]
        for copy in copies:
            copy.start()
        total[...] = jnp.zeros_like(total)
        for copy in copies:
            copy.wait()
        rows = tail[...].reshape(count * pad_rows, HALF)
        for part in range(2):
            pick = virtual_pick(count, virtual_rows, pad_rows, part)
            table[virtual_at, pl.ds(part * BLK, BLK), :] = dot(pick, rows).astype(jnp.bfloat16)

        @pl.loop(0, virtual_at + 1)
        def _(i):
            for part in range(2):
                rows = pl.ds(part * BLK, BLK)
                flipped[i, rows, :] = flip(table[i, rows, :])

    query = query_ref[...] * jnp.asarray(HEAD**-0.5, jnp.bfloat16)
    cotangent = grad_ref[...]
    cotangent_t = flip(cotangent)
    query_cols = heads_on_lanes(flip(query))
    query_rows = heads_on_rows(query)
    grad_cols = heads_on_lanes(cotangent_t)
    grad_rows = heads_on_rows(cotangent)

    listed = [chosen_ref[step, j] for j in range(LOC + XF + XG)]
    groups = [listed[j : j + 4] for j in range(0, LOC + XF + XG, 4)] + [[virtual_at]]
    slot_group = len(groups) - 2
    K = pl.ds(0, BLK)
    V = pl.ds(BLK, BLK)

    def rows_of(group, part):
        return jnp.concatenate([table[i, part, :] for i in group], axis=0)

    def flipped_of(number, part):
        group = groups[number]
        if number == slot_group:
            return jnp.concatenate([flip(table[i, part, :]) for i in group], axis=1)
        return jnp.concatenate([flipped[i, part, :] for i in group], axis=1)

    def deposit(number, part, terms):
        for at, i in enumerate(groups[number]):
            term = terms[at * BLK : (at + 1) * BLK]
            if number == slot_group:
                slot = i - slots_at
                start = pl.multiple_of(slot // count * PAIR, PAIR) + part * BLK
                pay_out[slot % count, pl.ds(start, BLK), :] = term.astype(jnp.bfloat16)
            else:
                total[i, pl.ds(part * BLK, BLK), :] += term

    spans, tops, sums = [], [], []
    start = 0
    for number, group in enumerate(groups):
        span = pl.ds(start, len(group) * BLK)
        start += len(group) * BLK
        scores = dot(rows_of(group, K), query_cols)
        top = jnp.max(scores, axis=0, keepdims=True)
        powers = jnp.exp(scores - top)
        scratch[span, :] = powers
        spans.append(span)
        tops.append(top)
        sums.append(jnp.sum(powers, axis=0, keepdims=True))
    peak = functools.reduce(jnp.maximum, tops)
    factors = [jnp.exp(top - peak) for top in tops]
    norm = 1.0 / functools.reduce(lambda a, b: a + b, [f * s for f, s in zip(factors, sums)])
    factors = [f * norm for f in factors]

    target_wide = jnp.zeros((HALF, 2 * BLK), jnp.float32)
    for number, group in enumerate(groups):
        low = (scratch[spans[number], :] * factors[number]).astype(jnp.bfloat16)
        target_wide += dot(flipped_of(number, V), low)
        deposit(number, 1, dot(low, grad_rows))
    target = own_head(target_wide).astype(jnp.bfloat16)
    target_ref[...] = flip(target)
    product = cotangent_t.astype(jnp.float32) * target.astype(jnp.float32)
    row_dot = jnp.concatenate(
        [
            jnp.sum(product[:HEAD], axis=0, keepdims=True),
            jnp.sum(product[HEAD:], axis=0, keepdims=True),
        ],
        axis=1,
    )

    query_wide = jnp.zeros((HALF, 2 * BLK), jnp.float32)
    for number, group in enumerate(groups):
        weights = scratch[spans[number], :] * factors[number]
        grad_weights = dot(rows_of(group, V), grad_cols)
        grad_scores = (weights * (grad_weights - row_dot)).astype(jnp.bfloat16)
        query_wide += dot(flipped_of(number, K), grad_scores)
        deposit(number, 0, dot(grad_scores, query_rows))
    query_grad_ref[...] = own_head(query_wide).T * (HEAD**-0.5)

    @pl.when(step == pl.num_programs(0) - 1)
    def _():
        below_out[...] = total[pl.ds(0, HB)].astype(jnp.bfloat16)
        own_out[...] = total[pl.ds(HB, own_blocks)]
        above_out[...] = total[pl.ds(HB + own_blocks, HB)].astype(jnp.bfloat16)
        for k, far_out in enumerate(far_outs):
            far_out[...] = total[pl.ds(far_start + k * own_blocks, own_blocks)].astype(
                jnp.bfloat16
            )
        rows = jnp.zeros((count * pad_rows, HALF), jnp.float32)
        for part in range(2):
            pick = virtual_pick(count, virtual_rows, pad_rows, part)
            low = total[virtual_at, pl.ds(part * BLK, BLK), :].astype(jnp.bfloat16)
            rows += lax.dot_general(
                pick, low, (((0,), (0,)), ((), ())), preferred_element_type=jnp.float32
            )
        pay_out[:, pl.ds(capacity * PAIR, pad_rows), :] = rows.astype(jnp.bfloat16).reshape(
            count, pad_rows, HALF
        )


def attend(half, sizes, chosen, node_query, cotangent, own, below, above, far, pay, earlier):
    own_blocks, far_count, count, capacity, virtual_rows, pad_rows = sizes
    rows = node_query.shape[0]
    kept = own_blocks + 2 * HB + far_count * own_blocks + 1
    listed = LOC + XF + XG
    column = pl.BlockSpec((BLK, HALF), lambda i: (i, half))
    anywhere = pl.BlockSpec(memory_space=pl.ANY)

    def whole(shape):
        return pl.BlockSpec(shape, lambda i: (0,) * len(shape))

    def body(*refs):
        refs = list(refs)
        inputs, refs = refs[: 7 + far_count], refs[7 + far_count + len(earlier) :]
        chosen_ref, query_ref, grad_ref, own_ref, below_ref, above_ref = inputs[:6]
        outs, scratch = refs[: 6 + far_count], refs[6 + far_count :]
        attend_kernel(
            sizes,
            chosen_ref,
            query_ref,
            grad_ref,
            own_ref,
            below_ref,
            above_ref,
            inputs[6:-1],
            inputs[-1],
            *outs[:5],
            outs[5:-1],
            outs[-1],
            *scratch,
        )

    block_shape = (own_blocks, PAIR, HALF)
    pay_shape = pay.shape
    results = pl.pallas_call(
        body,
        grid=(own_blocks,),
        out_shape=[
            jax.ShapeDtypeStruct((rows, FEAT), jnp.bfloat16),
            jax.ShapeDtypeStruct((rows, FEAT), jnp.float32),
            jax.ShapeDtypeStruct(block_shape, jnp.float32),
            jax.ShapeDtypeStruct(block_shape, jnp.bfloat16),
            jax.ShapeDtypeStruct(block_shape, jnp.bfloat16),
            *[jax.ShapeDtypeStruct(block_shape, jnp.bfloat16) for _ in far],
            jax.ShapeDtypeStruct(pay_shape, jnp.bfloat16),
        ],
        in_specs=[pl.BlockSpec(memory_space=pltpu.SMEM), column, column]
        + [anywhere] * (4 + far_count + len(earlier)),
        out_specs=[column, column, *[whole(block_shape)] * (3 + far_count), whole(pay_shape)],
        scratch_shapes=[
            pltpu.VMEM((kept + count * capacity, PAIR, HALF), jnp.bfloat16),
            pltpu.VMEM((kept, PAIR, HALF), jnp.bfloat16),
            pltpu.VMEM((count, pad_rows, HALF), jnp.bfloat16),
            pltpu.VMEM((kept, PAIR, HALF), jnp.float32),
            pltpu.VMEM(((listed + 1) * BLK, 2 * BLK), jnp.float32),
            pltpu.SemaphoreType.DMA((4 + far_count + capacity,)),
        ],
        input_output_aliases={7 + far_count + i: i for i in range(len(earlier))},
        compiler_params=pltpu.CompilerParams(
            vmem_limit_bytes=VMEM_LIMIT, dimension_semantics=("arbitrary",)
        ),
        cost_estimate=pl.CostEstimate(
            flops=12 * rows * (listed + 1) * BLK * HALF * 2,
            bytes_accessed=20 * 1024 * 1024,
            transcendentals=rows * (listed + 1) * BLK * 2,
        ),
    )(chosen, node_query, cotangent, own, below, above, *far, pay, *earlier)
    return results[:2], results[2], results[3], results[4], results[5:-1], results[-1]


def settle_kernel(
    sizes, wanted_ref, own_ref, below_ref, above_ref, far_refs, pay_ref, key_out, value_out, virtual_out
):
    own_blocks, _, count, capacity, virtual_rows, pad_rows = sizes
    step = pl.program_id(0)
    sums = own_ref[0]
    for ref in (below_ref, above_ref, *far_refs):
        sums += ref[0].astype(jnp.float32)
    key_out[...] = sums[:BLK]
    value_out[...] = sums[BLK:]

    for device in range(count):
        for slot in range(capacity):

            @pl.when(wanted_ref[device, slot] == step + 1)
            def _():
                term = pay_ref[device, pl.ds(slot * PAIR, PAIR), :].astype(jnp.float32)
                key_out[...] += term[:BLK]
                value_out[...] += term[BLK:]

    @pl.when(step == 0)
    def _():
        tail = pay_ref[:, pl.ds(capacity * PAIR, pad_rows), :].astype(jnp.float32)
        virtual_out[...] = jnp.sum(tail, axis=0)


def settle(half, sizes, wanted, own, below, above, far, pay, earlier):
    own_blocks, far_count, count, capacity, virtual_rows, pad_rows = sizes
    rows = own_blocks * BLK
    column = pl.BlockSpec((BLK, HALF), lambda i: (i, half))
    block = pl.BlockSpec((1, PAIR, HALF), lambda i: (i, 0, 0))

    def body(*refs):
        refs = list(refs)
        inputs, outs = refs[: 5 + far_count], refs[5 + far_count + len(earlier) :]
        settle_kernel(sizes, *inputs[:4], inputs[4:-1], inputs[-1], *outs)

    results = pl.pallas_call(
        body,
        grid=(own_blocks,),
        out_shape=[
            jax.ShapeDtypeStruct((rows, FEAT), jnp.float32),
            jax.ShapeDtypeStruct((rows, FEAT), jnp.float32),
            jax.ShapeDtypeStruct((pad_rows, HALF), jnp.float32),
        ],
        in_specs=[pl.BlockSpec(memory_space=pltpu.SMEM)]
        + [block] * (3 + far_count)
        + [pl.BlockSpec(pay.shape, lambda i: (0, 0, 0))]
        + [pl.BlockSpec(memory_space=pl.ANY)] * len(earlier),
        out_specs=[column, column, pl.BlockSpec((pad_rows, HALF), lambda i: (0, 0))],
        input_output_aliases={5 + far_count + i: i for i in range(len(earlier))},
        compiler_params=pltpu.CompilerParams(
            vmem_limit_bytes=VMEM_LIMIT, dimension_semantics=("arbitrary",)
        ),
    )(wanted, own, below, above, *far, pay, *earlier)
    return results[:2], results[2]


def per_device(
    node_query,
    node_key,
    node_value,
    cotangent,
    virtual_key,
    virtual_value,
    local_blocks,
    expander_dev,
    expander_pos,
    far_group,
    far_pos,
):
    count = lax.axis_size("dev")
    dom_count = lax.axis_size("dom")
    member = lax.axis_index("dev")
    own_blocks = local_blocks.shape[0]
    group_blocks = count * own_blocks
    virtual_rows = virtual_key.shape[0]
    pad_rows = -(-2 * virtual_rows // 16) * 16
    capacity = max(2, -(-(own_blocks * XG) // count))
    far_count = dom_count - 1
    sizes = (own_blocks, far_count, count, capacity, virtual_rows, pad_rows)

    flat_dev = expander_dev.reshape(-1)
    flat_pos = expander_pos.reshape(-1)
    order = jnp.arange(flat_dev.shape[0])
    same = flat_dev[:, None] == flat_dev[None, :]
    rank = jnp.sum((same & (order[None, :] < order[:, None])).astype(jnp.int32), axis=1)
    places = jnp.arange(count * capacity)
    hit = (flat_dev * capacity + rank)[None, :] == places[:, None]
    requests = jnp.sum(jnp.where(hit, flat_pos[None, :] + 1, 0), axis=1).astype(jnp.int32)
    wanted = lax.all_to_all(
        requests.reshape(count, capacity), "dev", split_axis=0, concat_axis=0, tiled=True
    )

    far_start = own_blocks + 2 * HB
    slots_at = far_start + far_count * own_blocks + 1
    chosen = jnp.concatenate(
        [
            (local_blocks % group_blocks - member * own_blocks + HB) % group_blocks,
            far_start + (far_group - 1) * own_blocks + far_pos,
            slots_at + (rank * count + flat_dev).reshape(own_blocks, XG),
        ],
        axis=1,
    ).astype(jnp.int32)

    halves = []
    for half in range(2):
        columns = slice(half * HALF, (half + 1) * HALF)
        own = jnp.concatenate(
            [
                node_key[:, columns].reshape(own_blocks, BLK, HALF),
                node_value[:, columns].reshape(own_blocks, BLK, HALF),
            ],
            axis=1,
        )
        tail = jnp.concatenate(
            [
                virtual_key[:, columns],
                virtual_value[:, columns],
                jnp.zeros((pad_rows - 2 * virtual_rows, HALF), jnp.bfloat16),
            ],
            axis=0,
        )
        below = shifted(own, "dev", 1)
        above = shifted(own, "dev", -1)
        far = [shifted(own, "dom", -k) for k in range(1, dom_count)]
        reply = make_reply(wanted, own, tail, capacity)
        pay = lax.all_to_all(reply, "dev", split_axis=0, concat_axis=0, tiled=True)
        halves.append((own, below, above, far, pay))

    results = ()
    parts = []
    for half, (own, below, above, far, pay) in enumerate(halves):
        results, own_sum, below_sum, above_sum, far_sums, pay_sum = attend(
            half, sizes, chosen, node_query, cotangent, own, below, above, far, pay, results
        )
        from_above = shifted(below_sum, "dev", -1)
        from_below = shifted(above_sum, "dev", 1)
        far_back = [shifted(term, "dom", k + 1) for k, term in enumerate(far_sums)]
        returned = lax.all_to_all(pay_sum, "dev", split_axis=0, concat_axis=0, tiled=True)
        parts.append((own_sum, from_below, from_above, far_back, returned))

    grads = ()
    tails = []
    for half, part in enumerate(parts):
        grads, tail = settle(half, sizes, wanted, *part, grads)
        tails.append(tail)
    virtual = jnp.concatenate(tails, axis=1)
    return (
        *results,
        *grads,
        virtual[:virtual_rows],
        virtual[virtual_rows : 2 * virtual_rows],
    )


def solution(mesh):
    spec = P(("dom", "dev"), None)
    return jax.shard_map(
        per_device, mesh=mesh, in_specs=(spec,) * 11, out_specs=(spec,) * 6, check_vma=False
    )
```

```python
import functools

import jax
import jax.numpy as jnp
from jax import lax
from jax.experimental import pallas as pl
from jax.experimental.pallas import tpu as pltpu
from jax.sharding import PartitionSpec as P

HB = 8
XG = 4
XF = 4
LOC = 16
BLK = 128
HEAD = 64
FEAT = 256
HALF = 128
PAIR = 2 * BLK
VMEM_LIMIT = 56 * 1024 * 1024


def shifted(value, axis, steps):
    count = lax.axis_size(axis)
    return lax.ppermute(value, axis, [(i, (i + steps) % count) for i in range(count)])


def dot(a, b):
    return jnp.dot(a, b, preferred_element_type=jnp.float32)


def flip(tile):
    return tile.astype(jnp.float32).T.astype(tile.dtype)


def heads_on_lanes(tile_t):
    row = lax.broadcasted_iota(jnp.int32, tile_t.shape, 0)
    zero = jnp.zeros_like(tile_t)
    return jnp.concatenate(
        [jnp.where(row < HEAD, tile_t, zero), jnp.where(row >= HEAD, tile_t, zero)], axis=1
    )


def heads_on_rows(tile):
    column = lax.broadcasted_iota(jnp.int32, tile.shape, 1)
    zero = jnp.zeros_like(tile)
    return jnp.concatenate(
        [jnp.where(column < HEAD, tile, zero), jnp.where(column >= HEAD, tile, zero)], axis=0
    )


def own_head(wide):
    return jnp.concatenate([wide[:HEAD, :BLK], wide[HEAD:, BLK:]], axis=0)


def virtual_pick(count, virtual_rows, pad_rows, part):
    shape = (count * virtual_rows, count * pad_rows)
    node = lax.broadcasted_iota(jnp.int32, shape, 0)
    place = lax.broadcasted_iota(jnp.int32, shape, 1)
    wanted = node // virtual_rows * pad_rows + part * virtual_rows + node % virtual_rows
    return (wanted == place).astype(jnp.bfloat16)


def reply_kernel(capacity, half, wanted_ref, kv_ref, virtual_ref, pay_ref, tail, sems, tail_sem):
    count = pay_ref.shape[0]
    columns = pl.ds(half * HALF, HALF)
    tail[...] = jnp.broadcast_to(virtual_ref[:, columns][None], tail.shape)
    tail_copy = pltpu.make_async_copy(
        tail, pay_ref.at[:, pl.ds(capacity * PAIR, tail.shape[1]), :], tail_sem
    )
    tail_copy.start()
    copies = []
    for device in range(count):
        for slot in range(capacity):
            position = jnp.clip(wanted_ref[device, slot] - 1, 0, kv_ref.shape[0] - 1)
            copies.append(
                pltpu.make_async_copy(
                    kv_ref.at[position, :, columns],
                    pay_ref.at[device, pl.ds(slot * PAIR, PAIR), :],
                    sems.at[device * capacity + slot],
                )
            )
            copies[-1].start()
    for copy in copies:
        copy.wait()
    tail_copy.wait()


def make_reply(half, wanted, kv, virtual_rows, capacity):
    count = wanted.shape[0]
    rows = virtual_rows.shape[0]
    return pl.pallas_call(
        functools.partial(reply_kernel, capacity, half),
        out_shape=jax.ShapeDtypeStruct((count, capacity * PAIR + rows, HALF), jnp.bfloat16),
        in_specs=[
            pl.BlockSpec(memory_space=pltpu.SMEM),
            pl.BlockSpec(memory_space=pltpu.VMEM),
            pl.BlockSpec(memory_space=pltpu.VMEM),
        ],
        out_specs=pl.BlockSpec(memory_space=pl.ANY),
        scratch_shapes=[
            pltpu.VMEM((count, rows, HALF), jnp.bfloat16),
            pltpu.SemaphoreType.DMA((count * capacity,)),
            pltpu.SemaphoreType.DMA,
        ],
        compiler_params=pltpu.CompilerParams(vmem_limit_bytes=VMEM_LIMIT),
    )(wanted, kv, virtual_rows)


def attend_kernel(
    sizes,
    half,
    chosen_ref,
    query_ref,
    grad_ref,
    own_ref,
    below_ref,
    above_ref,
    far_refs,
    pay_ref,
    target_ref,
    query_grad_ref,
    own_out,
    below_out,
    above_out,
    far_outs,
    pay_out,
    table,
    flipped,
    tail,
    total,
    scratch,
    sems,
):
    own_blocks, far_count, count, capacity, virtual_rows, pad_rows = sizes
    far_start = own_blocks + 2 * HB
    virtual_at = far_start + far_count * own_blocks
    slots_at = virtual_at + 1
    step = pl.program_id(0)

    @pl.when(step == 0)
    def _():
        columns = pl.ds(half * HALF, HALF)
        moves = [
            (below_ref.at[:, :, columns], table.at[pl.ds(0, HB)]),
            (own_ref.at[:, :, columns], table.at[pl.ds(HB, own_blocks)]),
            (above_ref.at[:, :, columns], table.at[pl.ds(HB + own_blocks, HB)]),
        ]
        for k, far_ref in enumerate(far_refs):
            moves.append((far_ref.at[:, :, columns], table.at[pl.ds(far_start + k * own_blocks, own_blocks)]))
        for slot in range(capacity):
            moves.append(
                (
                    pay_ref.at[:, pl.ds(slot * PAIR, PAIR), :],
                    table.at[pl.ds(slots_at + slot * count, count)],
                )
            )
        moves.append((pay_ref.at[:, pl.ds(capacity * PAIR, pad_rows), :], tail))
        copies = [
            pltpu.make_async_copy(source, target, sems.at[i])
            for i, (source, target) in enumerate(moves)
        ]
        for copy in copies:
            copy.start()
        total[...] = jnp.zeros_like(total)
        for copy in copies:
            copy.wait()
        rows = tail[...].reshape(count * pad_rows, HALF)
        for part in range(2):
            pick = virtual_pick(count, virtual_rows, pad_rows, part)
            table[virtual_at, pl.ds(part * BLK, BLK), :] = dot(pick, rows).astype(jnp.bfloat16)

        @pl.loop(0, virtual_at + 1)
        def _(i):
            for part in range(2):
                rows = pl.ds(part * BLK, BLK)
                flipped[i, rows, :] = flip(table[i, rows, :])

    query = query_ref[...] * jnp.asarray(HEAD**-0.5, jnp.bfloat16)
    cotangent = grad_ref[...]
    cotangent_t = flip(cotangent)
    query_cols = heads_on_lanes(flip(query))
    query_rows = heads_on_rows(query)
    grad_cols = heads_on_lanes(cotangent_t)
    grad_rows = heads_on_rows(cotangent)

    listed = [chosen_ref[step, j] for j in range(LOC + XF + XG)]
    groups = [listed[j : j + 4] for j in range(0, LOC + XF + XG, 4)] + [[virtual_at]]
    slot_group = len(groups) - 2
    K = pl.ds(0, BLK)
    V = pl.ds(BLK, BLK)

    def rows_of(group, part):
        return jnp.concatenate([table[i, part, :] for i in group], axis=0)

    def flipped_of(number, part):
        group = groups[number]
        if number == slot_group:
            return jnp.concatenate([flip(table[i, part, :]) for i in group], axis=1)
        return jnp.concatenate([flipped[i, part, :] for i in group], axis=1)

    def deposit(number, part, terms):
        for at, i in enumerate(groups[number]):
            term = terms[at * BLK : (at + 1) * BLK]
            if number == slot_group:
                slot = i - slots_at
                start = pl.multiple_of(slot // count * PAIR, PAIR) + part * BLK
                pay_out[slot % count, pl.ds(start, BLK), :] = term.astype(jnp.bfloat16)
            else:
                total[i, pl.ds(part * BLK, BLK), :] += term

    spans, tops, sums = [], [], []
    start = 0
    for number, group in enumerate(groups):
        span = pl.ds(start, len(group) * BLK)
        start += len(group) * BLK
        scores = dot(rows_of(group, K), query_cols)
        top = jnp.max(scores, axis=0, keepdims=True)
        powers = jnp.exp(scores - top)
        scratch[span, :] = powers
        spans.append(span)
        tops.append(top)
        sums.append(jnp.sum(powers, axis=0, keepdims=True))
    peak = functools.reduce(jnp.maximum, tops)
    factors = [jnp.exp(top - peak) for top in tops]
    norm = 1.0 / functools.reduce(lambda a, b: a + b, [f * s for f, s in zip(factors, sums)])
    factors = [f * norm for f in factors]

    target_wide = jnp.zeros((HALF, 2 * BLK), jnp.float32)
    for number, group in enumerate(groups):
        low = (scratch[spans[number], :] * factors[number]).astype(jnp.bfloat16)
        target_wide += dot(flipped_of(number, V), low)
        deposit(number, 1, dot(low, grad_rows))
    target = own_head(target_wide).astype(jnp.bfloat16)
    target_ref[...] = flip(target)
    product = cotangent_t.astype(jnp.float32) * target.astype(jnp.float32)
    row_dot = jnp.concatenate(
        [
            jnp.sum(product[:HEAD], axis=0, keepdims=True),
            jnp.sum(product[HEAD:], axis=0, keepdims=True),
        ],
        axis=1,
    )

    query_wide = jnp.zeros((HALF, 2 * BLK), jnp.float32)
    for number, group in enumerate(groups):
        weights = scratch[spans[number], :] * factors[number]
        grad_weights = dot(rows_of(group, V), grad_cols)
        grad_scores = (weights * (grad_weights - row_dot)).astype(jnp.bfloat16)
        query_wide += dot(flipped_of(number, K), grad_scores)
        deposit(number, 0, dot(grad_scores, query_rows))
    query_grad_ref[...] = own_head(query_wide).T * (HEAD**-0.5)

    @pl.when(step == pl.num_programs(0) - 1)
    def _():
        below_out[...] = total[pl.ds(0, HB)].astype(jnp.bfloat16)
        own_out[...] = total[pl.ds(HB, own_blocks)]
        above_out[...] = total[pl.ds(HB + own_blocks, HB)].astype(jnp.bfloat16)
        for k, far_out in enumerate(far_outs):
            far_out[...] = total[pl.ds(far_start + k * own_blocks, own_blocks)].astype(
                jnp.bfloat16
            )
        rows = jnp.zeros((count * pad_rows, HALF), jnp.float32)
        for part in range(2):
            pick = virtual_pick(count, virtual_rows, pad_rows, part)
            low = total[virtual_at, pl.ds(part * BLK, BLK), :].astype(jnp.bfloat16)
            rows += lax.dot_general(
                pick, low, (((0,), (0,)), ((), ())), preferred_element_type=jnp.float32
            )
        pay_out[:, pl.ds(capacity * PAIR, pad_rows), :] = rows.astype(jnp.bfloat16).reshape(
            count, pad_rows, HALF
        )


def attend(half, sizes, chosen, node_query, cotangent, own, below, above, far, pay, earlier):
    own_blocks, far_count, count, capacity, virtual_rows, pad_rows = sizes
    rows = node_query.shape[0]
    kept = own_blocks + 2 * HB + far_count * own_blocks + 1
    listed = LOC + XF + XG
    column = pl.BlockSpec((BLK, HALF), lambda i: (i, half))
    anywhere = pl.BlockSpec(memory_space=pl.ANY)

    def whole(shape):
        return pl.BlockSpec(shape, lambda i: (0,) * len(shape))

    def body(*refs):
        refs = list(refs)
        inputs, refs = refs[: 7 + far_count], refs[7 + far_count + len(earlier) :]
        chosen_ref, query_ref, grad_ref, own_ref, below_ref, above_ref = inputs[:6]
        outs, scratch = refs[: 6 + far_count], refs[6 + far_count :]
        attend_kernel(
            sizes,
            half,
            chosen_ref,
            query_ref,
            grad_ref,
            own_ref,
            below_ref,
            above_ref,
            inputs[6:-1],
            inputs[-1],
            *outs[:5],
            outs[5:-1],
            outs[-1],
            *scratch,
        )

    block_shape = (own_blocks, PAIR, HALF)
    pay_shape = pay.shape
    results = pl.pallas_call(
        body,
        grid=(own_blocks,),
        out_shape=[
            jax.ShapeDtypeStruct((rows, FEAT), jnp.bfloat16),
            jax.ShapeDtypeStruct((rows, FEAT), jnp.float32),
            jax.ShapeDtypeStruct(block_shape, jnp.float32),
            jax.ShapeDtypeStruct(block_shape, jnp.bfloat16),
            jax.ShapeDtypeStruct(block_shape, jnp.bfloat16),
            *[jax.ShapeDtypeStruct(block_shape, jnp.bfloat16) for _ in far],
            jax.ShapeDtypeStruct(pay_shape, jnp.bfloat16),
        ],
        in_specs=[pl.BlockSpec(memory_space=pltpu.SMEM), column, column]
        + [anywhere] * (4 + far_count + len(earlier)),
        out_specs=[column, column, *[whole(block_shape)] * (3 + far_count), whole(pay_shape)],
        scratch_shapes=[
            pltpu.VMEM((kept + count * capacity, PAIR, HALF), jnp.bfloat16),
            pltpu.VMEM((kept, PAIR, HALF), jnp.bfloat16),
            pltpu.VMEM((count, pad_rows, HALF), jnp.bfloat16),
            pltpu.VMEM((kept, PAIR, HALF), jnp.float32),
            pltpu.VMEM(((listed + 1) * BLK, 2 * BLK), jnp.float32),
            pltpu.SemaphoreType.DMA((4 + far_count + capacity,)),
        ],
        input_output_aliases={7 + far_count + i: i for i in range(len(earlier))},
        compiler_params=pltpu.CompilerParams(
            vmem_limit_bytes=VMEM_LIMIT, dimension_semantics=("arbitrary",)
        ),
        cost_estimate=pl.CostEstimate(
            flops=12 * rows * (listed + 1) * BLK * HALF * 2,
            bytes_accessed=20 * 1024 * 1024,
            transcendentals=rows * (listed + 1) * BLK * 2,
        ),
    )(chosen, node_query, cotangent, own, below, above, *far, pay, *earlier)
    return results[:2], results[2], results[3], results[4], results[5:-1], results[-1]


def settle_kernel(
    sizes, wanted_ref, own_ref, below_ref, above_ref, far_refs, pay_ref, key_out, value_out, virtual_out, total
):
    own_blocks, _, count, capacity, virtual_rows, pad_rows = sizes
    sums = own_ref[...]
    for ref in (below_ref, above_ref, *far_refs):
        sums += ref[...].astype(jnp.float32)
    total[...] = sums

    @pl.loop(0, count)
    def _(device):
        for slot in range(capacity):
            place = wanted_ref[device, slot]

            @pl.when(place > 0)
            def _():
                term = pay_ref[device, pl.ds(slot * PAIR, PAIR), :].astype(jnp.float32)
                total[jnp.maximum(place - 1, 0)] += term

    sums = total[...]
    key_out[...] = sums[:, :BLK].reshape(key_out.shape)
    value_out[...] = sums[:, BLK:].reshape(value_out.shape)
    tail = pay_ref[:, pl.ds(capacity * PAIR, pad_rows), :].astype(jnp.float32)
    virtual_out[...] = jnp.sum(tail, axis=0)


def settle(half, sizes, wanted, own, below, above, far, pay, earlier):
    own_blocks, far_count, count, capacity, virtual_rows, pad_rows = sizes
    rows = own_blocks * BLK
    column = pl.BlockSpec((rows, HALF), lambda i: (0, half))
    block = pl.BlockSpec((own_blocks, PAIR, HALF), lambda i: (0, 0, 0))

    def body(*refs):
        refs = list(refs)
        inputs, outs = refs[: 5 + far_count], refs[5 + far_count + len(earlier) :]
        settle_kernel(sizes, *inputs[:4], inputs[4:-1], inputs[-1], *outs)

    results = pl.pallas_call(
        body,
        grid=(1,),
        out_shape=[
            jax.ShapeDtypeStruct((rows, FEAT), jnp.float32),
            jax.ShapeDtypeStruct((rows, FEAT), jnp.float32),
            jax.ShapeDtypeStruct((pad_rows, HALF), jnp.float32),
        ],
        in_specs=[pl.BlockSpec(memory_space=pltpu.SMEM)]
        + [block] * (3 + far_count)
        + [pl.BlockSpec(pay.shape, lambda i: (0, 0, 0))]
        + [pl.BlockSpec(memory_space=pl.ANY)] * len(earlier),
        out_specs=[column, column, pl.BlockSpec((pad_rows, HALF), lambda i: (0, 0))],
        scratch_shapes=[pltpu.VMEM((own_blocks, PAIR, HALF), jnp.float32)],
        input_output_aliases={5 + far_count + i: i for i in range(len(earlier))},
        compiler_params=pltpu.CompilerParams(
            vmem_limit_bytes=VMEM_LIMIT, dimension_semantics=("arbitrary",)
        ),
    )(wanted, own, below, above, *far, pay, *earlier)
    return results[:2], results[2]


def per_device(
    node_query,
    node_key,
    node_value,
    cotangent,
    virtual_key,
    virtual_value,
    local_blocks,
    expander_dev,
    expander_pos,
    far_group,
    far_pos,
):
    count = lax.axis_size("dev")
    dom_count = lax.axis_size("dom")
    member = lax.axis_index("dev")
    own_blocks = local_blocks.shape[0]
    group_blocks = count * own_blocks
    virtual_rows = virtual_key.shape[0]
    pad_rows = -(-2 * virtual_rows // 16) * 16
    capacity = max(2, -(-(own_blocks * XG) // count))
    far_count = dom_count - 1
    sizes = (own_blocks, far_count, count, capacity, virtual_rows, pad_rows)

    flat_dev = expander_dev.reshape(-1)
    flat_pos = expander_pos.reshape(-1)
    order = jnp.arange(flat_dev.shape[0])
    same = flat_dev[:, None] == flat_dev[None, :]
    rank = jnp.sum((same & (order[None, :] < order[:, None])).astype(jnp.int32), axis=1)
    places = jnp.arange(count * capacity)
    hit = (flat_dev * capacity + rank)[None, :] == places[:, None]
    requests = jnp.sum(jnp.where(hit, flat_pos[None, :] + 1, 0), axis=1).astype(jnp.int32)
    wanted = lax.all_to_all(
        requests.reshape(count, capacity), "dev", split_axis=0, concat_axis=0, tiled=True
    )

    far_start = own_blocks + 2 * HB
    slots_at = far_start + far_count * own_blocks + 1
    chosen = jnp.concatenate(
        [
            (local_blocks % group_blocks - member * own_blocks + HB) % group_blocks,
            far_start + (far_group - 1) * own_blocks + far_pos,
            slots_at + (rank * count + flat_dev).reshape(own_blocks, XG),
        ],
        axis=1,
    ).astype(jnp.int32)

    own = jnp.concatenate(
        [
            node_key.reshape(own_blocks, BLK, FEAT),
            node_value.reshape(own_blocks, BLK, FEAT),
        ],
        axis=1,
    )
    tail = jnp.concatenate(
        [
            virtual_key,
            virtual_value,
            jnp.zeros((pad_rows - 2 * virtual_rows, FEAT), jnp.bfloat16),
        ],
        axis=0,
    )
    near = [
        shifted(own, "dev", 1),
        shifted(own, "dev", -1),
        *[shifted(own, "dom", -k) for k in range(1, dom_count)],
    ]
    replies = [make_reply(half, wanted, own, tail, capacity) for half in range(2)]
    pays = [lax.all_to_all(replies[0], "dev", split_axis=0, concat_axis=0, tiled=True)]
    near, second = lax.optimization_barrier((near, replies[1]))
    pays.append(lax.all_to_all(second, "dev", split_axis=0, concat_axis=0, tiled=True))
    below, above, *far = near

    results = ()
    parts = []
    for half, pay in enumerate(pays):
        results, own_sum, below_sum, above_sum, far_sums, pay_sum = attend(
            half, sizes, chosen, node_query, cotangent, own, below, above, far, pay, results
        )
        from_above = shifted(below_sum, "dev", -1)
        from_below = shifted(above_sum, "dev", 1)
        far_back = [shifted(term, "dom", k + 1) for k, term in enumerate(far_sums)]
        if parts:
            earlier_part, pay_sum = lax.optimization_barrier((parts[-1], pay_sum))
            parts[-1] = earlier_part
        returned = lax.all_to_all(pay_sum, "dev", split_axis=0, concat_axis=0, tiled=True)
        parts.append((own_sum, from_below, from_above, far_back, returned))

    grads = ()
    tails = []
    for half, part in enumerate(parts):
        grads, tail = settle(half, sizes, wanted, *part, grads)
        tails.append(tail)
    virtual = jnp.concatenate(tails, axis=1)
    return (
        *results,
        *grads,
        virtual[:virtual_rows],
        virtual[virtual_rows : 2 * virtual_rows],
    )


def solution(mesh):
    spec = P(("dom", "dev"), None)
    return jax.shard_map(
        per_device, mesh=mesh, in_specs=(spec,) * 11, out_specs=(spec,) * 6, check_vma=False
    )
```

```python
import functools

import jax
import jax.numpy as jnp
from jax import lax
from jax.experimental import pallas as pl
from jax.experimental.pallas import tpu as pltpu
from jax.sharding import PartitionSpec as P

HB = 8
XG = 4
XF = 4
LOC = 16
BLK = 128
HEAD = 64
FEAT = 256
HALF = 128
PAIR = 2 * BLK
VMEM_LIMIT = 56 * 1024 * 1024


def shifted(value, axis, steps):
    count = lax.axis_size(axis)
    return lax.ppermute(value, axis, [(i, (i + steps) % count) for i in range(count)])


def dot(a, b):
    return jnp.dot(a, b, preferred_element_type=jnp.float32)


def flip(tile):
    return tile.astype(jnp.float32).T.astype(tile.dtype)


def heads_on_lanes(tile_t):
    row = lax.broadcasted_iota(jnp.int32, tile_t.shape, 0)
    zero = jnp.zeros_like(tile_t)
    return jnp.concatenate(
        [jnp.where(row < HEAD, tile_t, zero), jnp.where(row >= HEAD, tile_t, zero)], axis=1
    )


def heads_on_rows(tile):
    column = lax.broadcasted_iota(jnp.int32, tile.shape, 1)
    zero = jnp.zeros_like(tile)
    return jnp.concatenate(
        [jnp.where(column < HEAD, tile, zero), jnp.where(column >= HEAD, tile, zero)], axis=0
    )


def own_head(wide):
    return jnp.concatenate([wide[:HEAD, :BLK], wide[HEAD:, BLK:]], axis=0)


def virtual_pick(count, virtual_rows, pad_rows, part):
    shape = (count * virtual_rows, count * pad_rows)
    node = lax.broadcasted_iota(jnp.int32, shape, 0)
    place = lax.broadcasted_iota(jnp.int32, shape, 1)
    wanted = node // virtual_rows * pad_rows + part * virtual_rows + node % virtual_rows
    return (wanted == place).astype(jnp.bfloat16)


def relay_kernel(half, asked_ref, held_ref, pay_ref, pieces):
    count, rows = held_ref.shape[0], held_ref.shape[1]
    own_blocks, piece = pieces.shape[0] // count, pieces.shape[1]

    @pl.loop(0, count)
    def _(owner):
        found = held_ref[owner, pl.ds(0, own_blocks * piece), :].astype(jnp.float32)
        pieces[pl.ds(owner * own_blocks, own_blocks)] = found.reshape(own_blocks, piece, HALF)

    @pl.loop(0, count)
    def _(device):
        for first in range(0, own_blocks * XG, 2):
            pair = [pieces[asked_ref[device, first + at]] for at in range(2)]
            pay_ref[device, pl.ds(first * piece, 2 * piece), :] = jnp.concatenate(
                pair, axis=0
            ).astype(jnp.bfloat16)


def relay(half, asked, held, own_blocks):
    count = held.shape[0]
    piece = PAIR // count
    return pl.pallas_call(
        functools.partial(relay_kernel, half),
        grid=(1,),
        out_shape=jax.ShapeDtypeStruct((count, own_blocks * XG * piece, HALF), jnp.bfloat16),
        in_specs=[
            pl.BlockSpec(memory_space=pltpu.SMEM),
            pl.BlockSpec(held.shape[:2] + (HALF,), lambda i: (0, 0, half)),
        ],
        out_specs=pl.BlockSpec((count, own_blocks * XG * piece, HALF), lambda i: (0, 0, 0)),
        scratch_shapes=[pltpu.VMEM((count * own_blocks, piece, HALF), jnp.float32)],
        compiler_params=pltpu.CompilerParams(vmem_limit_bytes=VMEM_LIMIT),
    )(asked, held)


def gather_kernel(asked_ref, back_ref, virtual_ref, out_ref, pieces):
    count = back_ref.shape[0]
    own_blocks, piece = pieces.shape[0] // count, pieces.shape[1]
    held = own_blocks * piece
    pieces[...] = jnp.zeros_like(pieces)

    @pl.loop(0, count)
    def _(device):
        for first in range(0, own_blocks * XG, XG):
            terms = back_ref[device, pl.ds(first * piece, XG * piece), :].astype(jnp.float32)
            places = [asked_ref[device, first + at] for at in range(XG)]
            sums = [pieces[place] for place in places]
            for at, place in enumerate(places):
                pieces[place] = sums[at] + terms[at * piece : (at + 1) * piece]

    @pl.loop(0, count)
    def _(owner):
        found = pieces[pl.ds(owner * own_blocks, own_blocks)].reshape(held, HALF)
        out_ref[owner, pl.ds(0, held), :] = found.astype(jnp.bfloat16)
        out_ref[owner, pl.ds(held, virtual_ref.shape[1]), :] = virtual_ref[owner]


def gather(half, asked, back, virtual, earlier):
    count, pad_rows = virtual.shape[0], virtual.shape[1]
    piece = PAIR // count
    own_blocks = back.shape[1] // (XG * piece)
    rows = own_blocks * piece + pad_rows

    def body(*refs):
        gather_kernel(*refs[:3], *refs[3 + len(earlier) :])

    return pl.pallas_call(
        body,
        grid=(1,),
        out_shape=jax.ShapeDtypeStruct((count, rows, FEAT), jnp.bfloat16),
        in_specs=[
            pl.BlockSpec(memory_space=pltpu.SMEM),
            pl.BlockSpec(back.shape, lambda i: (0, 0, 0)),
            pl.BlockSpec(virtual.shape, lambda i: (0, 0, 0)),
        ]
        + [pl.BlockSpec(memory_space=pl.ANY)] * len(earlier),
        out_specs=pl.BlockSpec((count, rows, HALF), lambda i: (0, 0, half)),
        scratch_shapes=[pltpu.VMEM((count * own_blocks, piece, HALF), jnp.float32)],
        input_output_aliases={3 + i: i for i in range(len(earlier))},
        compiler_params=pltpu.CompilerParams(vmem_limit_bytes=VMEM_LIMIT),
    )(asked, back, virtual, *earlier)


def attend_kernel(
    sizes,
    half,
    chosen_ref,
    query_ref,
    grad_ref,
    own_ref,
    below_ref,
    above_ref,
    far_refs,
    held_ref,
    pay_ref,
    target_ref,
    query_grad_ref,
    below_out,
    above_out,
    far_outs,
    own_out,
    virtual_out,
    pay_out,
    table,
    flipped,
    tail,
    asked,
    total,
    scratch,
    sems,
):
    own_blocks, far_count, count, virtual_rows, pad_rows = sizes
    piece = PAIR // count
    far_start = own_blocks + 2 * HB
    virtual_at = far_start + far_count * own_blocks
    slots_at = virtual_at + 1
    step = pl.program_id(0)

    @pl.when(step == 0)
    def _():
        columns = pl.ds(half * HALF, HALF)
        moves = [
            (below_ref.at[:, :, columns], table.at[pl.ds(0, HB)]),
            (own_ref.at[:, :, columns], table.at[pl.ds(HB, own_blocks)]),
            (above_ref.at[:, :, columns], table.at[pl.ds(HB + own_blocks, HB)]),
        ]
        for k, far_ref in enumerate(far_refs):
            moves.append((far_ref.at[:, :, columns], table.at[pl.ds(far_start + k * own_blocks, own_blocks)]))
        moves.append((pay_ref, asked))
        moves.append((held_ref.at[:, pl.ds(own_blocks * piece, pad_rows), columns], tail))
        copies = [
            pltpu.make_async_copy(source, target, sems.at[i])
            for i, (source, target) in enumerate(moves)
        ]
        for copy in copies:
            copy.start()
        total[...] = jnp.zeros_like(total)
        for copy in copies:
            copy.wait()
        rows = tail[...].reshape(count * pad_rows, HALF)
        for part in range(2):
            pick = virtual_pick(count, virtual_rows, pad_rows, part)
            table[virtual_at, pl.ds(part * BLK, BLK), :] = dot(pick, rows).astype(jnp.bfloat16)

        @pl.loop(0, count, step=2)
        def _(device):
            rows = pl.ds(pl.multiple_of(device * piece, 2 * piece), 2 * piece)
            for first in range(0, own_blocks * XG, 2):
                span = pl.ds(first * piece, 2 * piece)
                pair = [asked[device + at, span, :].astype(jnp.float32) for at in range(2)]
                for at in range(2):
                    part = slice(at * piece, (at + 1) * piece)
                    table[slots_at + first + at, rows, :] = jnp.concatenate(
                        [pair[0][part], pair[1][part]], axis=0
                    ).astype(jnp.bfloat16)

        @pl.loop(0, virtual_at + 1)
        def _(i):
            for part in range(2):
                rows = pl.ds(part * BLK, BLK)
                flipped[i, rows, :] = flip(table[i, rows, :])

    query = query_ref[...] * jnp.asarray(HEAD**-0.5, jnp.bfloat16)
    cotangent = grad_ref[...]
    cotangent_t = flip(cotangent)
    query_cols = heads_on_lanes(flip(query))
    query_rows = heads_on_rows(query)
    grad_cols = heads_on_lanes(cotangent_t)
    grad_rows = heads_on_rows(cotangent)

    listed = [chosen_ref[step, j] for j in range(LOC + XF)]
    listed += [slots_at + step * XG + j for j in range(XG)]
    groups = [listed[j : j + 4] for j in range(0, LOC + XF + XG, 4)] + [[virtual_at]]
    slot_group = len(groups) - 2
    K = pl.ds(0, BLK)
    V = pl.ds(BLK, BLK)

    def rows_of(group, part):
        return jnp.concatenate([table[i, part, :] for i in group], axis=0)

    def flipped_of(number, part):
        group = groups[number]
        if number == slot_group:
            return jnp.concatenate([flip(table[i, part, :]) for i in group], axis=1)
        return jnp.concatenate([flipped[i, part, :] for i in group], axis=1)

    def deposit(number, part, terms):
        if number != slot_group:
            for at, i in enumerate(groups[number]):
                total[i, pl.ds(part * BLK, BLK), :] += terms[at * BLK : (at + 1) * BLK]
            return
        for first in range(0, XG, 2):
            start = pl.multiple_of((step * XG + first) * piece, 2 * piece)
            for place in range(BLK // piece):
                rows = [
                    terms[at * BLK + place * piece : at * BLK + (place + 1) * piece]
                    for at in (first, first + 1)
                ]
                pay_out[part * (BLK // piece) + place, pl.ds(start, 2 * piece), :] = (
                    jnp.concatenate(rows, axis=0).astype(jnp.bfloat16)
                )

    spans, tops, sums = [], [], []
    start = 0
    for number, group in enumerate(groups):
        span = pl.ds(start, len(group) * BLK)
        start += len(group) * BLK
        scores = dot(rows_of(group, K), query_cols)
        top = jnp.max(scores, axis=0, keepdims=True)
        powers = jnp.exp(scores - top)
        scratch[span, :] = powers
        spans.append(span)
        tops.append(top)
        sums.append(jnp.sum(powers, axis=0, keepdims=True))
    peak = functools.reduce(jnp.maximum, tops)
    factors = [jnp.exp(top - peak) for top in tops]
    norm = 1.0 / functools.reduce(lambda a, b: a + b, [f * s for f, s in zip(factors, sums)])
    factors = [f * norm for f in factors]

    target_wide = jnp.zeros((HALF, 2 * BLK), jnp.float32)
    for number, group in enumerate(groups):
        low = (scratch[spans[number], :] * factors[number]).astype(jnp.bfloat16)
        target_wide += dot(flipped_of(number, V), low)
        deposit(number, 1, dot(low, grad_rows))
    target = own_head(target_wide).astype(jnp.bfloat16)
    target_ref[...] = flip(target)
    product = cotangent_t.astype(jnp.float32) * target.astype(jnp.float32)
    row_dot = jnp.concatenate(
        [
            jnp.sum(product[:HEAD], axis=0, keepdims=True),
            jnp.sum(product[HEAD:], axis=0, keepdims=True),
        ],
        axis=1,
    )

    query_wide = jnp.zeros((HALF, 2 * BLK), jnp.float32)
    for number, group in enumerate(groups):
        weights = scratch[spans[number], :] * factors[number]
        grad_weights = dot(rows_of(group, V), grad_cols)
        grad_scores = (weights * (grad_weights - row_dot)).astype(jnp.bfloat16)
        query_wide += dot(flipped_of(number, K), grad_scores)
        deposit(number, 0, dot(grad_scores, query_rows))
    query_grad_ref[...] = own_head(query_wide).T * (HEAD**-0.5)

    @pl.when(step == pl.num_programs(0) - 1)
    def _():
        below_out[...] = total[pl.ds(0, HB)].astype(jnp.bfloat16)
        own_out[...] = total[pl.ds(HB, own_blocks)]
        above_out[...] = total[pl.ds(HB + own_blocks, HB)].astype(jnp.bfloat16)
        for k, far_out in enumerate(far_outs):
            far_out[...] = total[pl.ds(far_start + k * own_blocks, own_blocks)].astype(
                jnp.bfloat16
            )
        rows = jnp.zeros((count * pad_rows, HALF), jnp.float32)
        for part in range(2):
            pick = virtual_pick(count, virtual_rows, pad_rows, part)
            low = total[virtual_at, pl.ds(part * BLK, BLK), :].astype(jnp.bfloat16)
            rows += lax.dot_general(
                pick, low, (((0,), (0,)), ((), ())), preferred_element_type=jnp.float32
            )
        virtual_out[...] = rows.astype(jnp.bfloat16).reshape(count, pad_rows, HALF)


def attend(half, sizes, chosen, node_query, cotangent, own, near, held, pay, earlier):
    own_blocks, far_count, count, virtual_rows, pad_rows = sizes
    rows = node_query.shape[0]
    kept = own_blocks + 2 * HB + far_count * own_blocks + 1
    listed = LOC + XF + XG
    column = pl.BlockSpec((BLK, HALF), lambda i: (i, half))
    anywhere = pl.BlockSpec(memory_space=pl.ANY)
    block_shape = (own_blocks, PAIR, HALF)
    virtual_shape = (count, pad_rows, HALF)
    wide = pl.BlockSpec(block_shape, lambda i: (0, 0, half))

    def whole(shape):
        return pl.BlockSpec(shape, lambda i: (0,) * len(shape))

    inputs = 6 + len(near)

    def body(*refs):
        refs = list(refs)
        given, refs = refs[:inputs], refs[inputs + len(earlier) :]
        outs, scratch = refs[: 5 + len(near)], refs[5 + len(near) :]
        attend_kernel(
            sizes,
            half,
            *given[:6],
            given[6:-2],
            *given[-2:],
            *outs[:4],
            outs[4:-3],
            *outs[-3:],
            *scratch,
        )

    results = pl.pallas_call(
        body,
        grid=(own_blocks,),
        out_shape=[
            jax.ShapeDtypeStruct((rows, FEAT), jnp.bfloat16),
            jax.ShapeDtypeStruct((rows, FEAT), jnp.float32),
            *[jax.ShapeDtypeStruct(own.shape, jnp.bfloat16) for _ in near],
            jax.ShapeDtypeStruct(block_shape, jnp.float32),
            jax.ShapeDtypeStruct(virtual_shape, jnp.bfloat16),
            jax.ShapeDtypeStruct(pay.shape, jnp.bfloat16),
        ],
        in_specs=[pl.BlockSpec(memory_space=pltpu.SMEM), column, column]
        + [anywhere] * (3 + len(near) + len(earlier)),
        out_specs=[column, column]
        + [wide] * len(near)
        + [whole(block_shape), whole(virtual_shape), whole(pay.shape)],
        scratch_shapes=[
            pltpu.VMEM((kept + own_blocks * XG, PAIR, HALF), jnp.bfloat16),
            pltpu.VMEM((kept, PAIR, HALF), jnp.bfloat16),
            pltpu.VMEM((count, pad_rows, HALF), jnp.bfloat16),
            pltpu.VMEM(pay.shape, jnp.bfloat16),
            pltpu.VMEM((kept, PAIR, HALF), jnp.float32),
            pltpu.VMEM(((listed + 1) * BLK, 2 * BLK), jnp.float32),
            pltpu.SemaphoreType.DMA((3 + len(near),)),
        ],
        input_output_aliases={inputs + i: i for i in range(len(earlier))},
        compiler_params=pltpu.CompilerParams(
            vmem_limit_bytes=VMEM_LIMIT, dimension_semantics=("arbitrary",)
        ),
        cost_estimate=pl.CostEstimate(
            flops=12 * rows * (listed + 1) * BLK * HALF * 2,
            bytes_accessed=20 * 1024 * 1024,
            transcendentals=rows * (listed + 1) * BLK * 2,
        ),
    )(chosen, node_query, cotangent, own, *near, held, pay, *earlier)
    return results[:-3], results[-3:]


def settle_kernel(sizes, sum_refs, back_ref, key_out, value_out, virtual_out, total):
    own_blocks, _, count, _, pad_rows = sizes
    piece = PAIR // count
    for half, sum_ref in enumerate(sum_refs):
        columns = pl.ds(half * HALF, HALF)
        total[...] = sum_ref[...]

        @pl.loop(0, count)
        def _(device):
            rows = pl.ds(pl.multiple_of(device * piece, piece), piece)
            back = back_ref[device, pl.ds(0, own_blocks * piece), columns].astype(jnp.float32)
            for block in range(own_blocks):
                total[block, rows, :] += back[block * piece : (block + 1) * piece]

        sums = total[...]
        key_out[:, columns] = sums[:, :BLK].reshape(own_blocks * BLK, HALF)
        value_out[:, columns] = sums[:, BLK:].reshape(own_blocks * BLK, HALF)
    tail = back_ref[:, pl.ds(own_blocks * piece, pad_rows), :].astype(jnp.float32)
    virtual_out[...] = jnp.sum(tail, axis=0)


def settle(sizes, sums, back):
    own_blocks, _, _, _, pad_rows = sizes
    rows = own_blocks * BLK

    def body(*refs):
        settle_kernel(sizes, refs[: len(sums)], *refs[len(sums) :])

    return pl.pallas_call(
        body,
        out_shape=[
            jax.ShapeDtypeStruct((rows, FEAT), jnp.float32),
            jax.ShapeDtypeStruct((rows, FEAT), jnp.float32),
            jax.ShapeDtypeStruct((pad_rows, FEAT), jnp.float32),
        ],
        in_specs=[pl.BlockSpec(memory_space=pltpu.VMEM)] * (len(sums) + 1),
        out_specs=[pl.BlockSpec(memory_space=pltpu.VMEM)] * 3,
        scratch_shapes=[pltpu.VMEM((own_blocks, PAIR, HALF), jnp.float32)],
        compiler_params=pltpu.CompilerParams(vmem_limit_bytes=VMEM_LIMIT),
    )(*sums, back)


def per_device(
    node_query,
    node_key,
    node_value,
    cotangent,
    virtual_key,
    virtual_value,
    local_blocks,
    expander_dev,
    expander_pos,
    far_group,
    far_pos,
):
    count = lax.axis_size("dev")
    dom_count = lax.axis_size("dom")
    member = lax.axis_index("dev")
    own_blocks = local_blocks.shape[0]
    group_blocks = count * own_blocks
    virtual_rows = virtual_key.shape[0]
    pad_rows = -(-(2 * virtual_rows + 1) // 16) * 16
    far_count = dom_count - 1
    piece = PAIR // count
    sizes = (own_blocks, far_count, count, virtual_rows, pad_rows)

    far_start = own_blocks + 2 * HB
    chosen = jnp.concatenate(
        [
            (local_blocks % group_blocks - member * own_blocks + HB) % group_blocks,
            far_start + (far_group - 1) * own_blocks + far_pos,
        ],
        axis=1,
    ).astype(jnp.int32)

    own = jnp.concatenate(
        [
            node_key.reshape(own_blocks, BLK, FEAT),
            node_value.reshape(own_blocks, BLK, FEAT),
        ],
        axis=1,
    )
    pieces = own.reshape(own_blocks, count, piece, FEAT).transpose(1, 0, 2, 3)
    numbers = (expander_dev * own_blocks + expander_pos).reshape(1, -1).astype(jnp.bfloat16)
    tail = jnp.concatenate(
        [
            virtual_key,
            virtual_value,
            jnp.pad(numbers, ((0, pad_rows - 2 * virtual_rows - 1), (0, FEAT - numbers.shape[1]))),
        ],
        axis=0,
    )
    spread = jnp.concatenate(
        [
            pieces.reshape(count, own_blocks * piece, FEAT),
            jnp.broadcast_to(tail[None], (count, pad_rows, FEAT)),
        ],
        axis=1,
    )
    held = lax.all_to_all(spread, "dev", split_axis=0, concat_axis=0, tiled=True)
    asked = held[:, own_blocks * piece + 2 * virtual_rows, : own_blocks * XG].astype(jnp.int32)
    near = [
        shifted(own, "dev", 1),
        shifted(own, "dev", -1),
        *[shifted(own, "dom", -k) for k in range(1, dom_count)],
    ]
    longest = 2 + far_count // 2
    held, asked, near[:longest], near[longest + 1 :] = lax.optimization_barrier(
        (held, asked, near[:longest], near[longest + 1 :])
    )
    sent = [relay(half, asked, held, own_blocks) for half in range(2)]
    pays = [lax.all_to_all(sent[0], "dev", split_axis=0, concat_axis=0, tiled=True)]
    near, second = lax.optimization_barrier((near, sent[1]))
    pays.append(lax.all_to_all(second, "dev", split_axis=0, concat_axis=0, tiled=True))

    results, gathered, own_sums = [], [], []
    for half, pay in enumerate(pays):
        results, (own_sum, virtual_sum, pay_sum) = attend(
            half, sizes, chosen, node_query, cotangent, own, near, held, pay, results
        )
        own_sums.append(own_sum)
        back = lax.all_to_all(pay_sum, "dev", split_axis=0, concat_axis=0, tiled=True)
        gathered = [gather(half, asked, back, virtual_sum, gathered)]

    returned = lax.all_to_all(gathered[0], "dev", split_axis=0, concat_axis=0, tiled=True)
    attended, query_grad, below_sum, above_sum, *far_sums = results
    near_back = [
        shifted(below_sum, "dev", -1),
        shifted(above_sum, "dev", 1),
        *[shifted(term, "dom", k + 1) for k, term in enumerate(far_sums)],
    ]
    sums = [
        own_sum
        + sum(term[:, :, half * HALF : (half + 1) * HALF].astype(jnp.float32) for term in near_back)
        for half, own_sum in enumerate(own_sums)
    ]
    key_grad, value_grad, virtual = settle(sizes, sums, returned)
    return (
        attended,
        query_grad,
        key_grad,
        value_grad,
        virtual[:virtual_rows],
        virtual[virtual_rows : 2 * virtual_rows],
    )


def solution(mesh):
    spec = P(("dom", "dev"), None)
    return jax.shard_map(
        per_device, mesh=mesh, in_specs=(spec,) * 11, out_specs=(spec,) * 6, check_vma=False
    )
```

```python
import functools

import jax
import jax.numpy as jnp
from jax import lax
from jax.experimental import pallas as pl
from jax.experimental.pallas import tpu as pltpu
from jax.sharding import PartitionSpec as P

HB = 8
XG = 4
XF = 4
LOC = 16
BLK = 128
HEAD = 64
FEAT = 256
HALF = 128
PAIR = 2 * BLK
BLOCKS_AT_ONCE = 4
STEPS = 4
VMEM_LIMIT = 56 * 1024 * 1024


def shifted(value, axis, steps):
    count = lax.axis_size(axis)
    return lax.ppermute(value, axis, [(i, (i + steps) % count) for i in range(count)])


def dot(a, b):
    return jnp.dot(a, b, preferred_element_type=jnp.float32)


def flip(tile):
    return tile.T


def heads_on_lanes(tile_t):
    row = lax.broadcasted_iota(jnp.int32, tile_t.shape, 0)
    zero = jnp.zeros_like(tile_t)
    return jnp.concatenate(
        [jnp.where(row < HEAD, tile_t, zero), jnp.where(row >= HEAD, tile_t, zero)], axis=1
    )


def heads_on_rows(tile):
    column = lax.broadcasted_iota(jnp.int32, tile.shape, 1)
    zero = jnp.zeros_like(tile)
    return jnp.concatenate(
        [jnp.where(column < HEAD, tile, zero), jnp.where(column >= HEAD, tile, zero)], axis=0
    )


def own_head(wide):
    return jnp.concatenate([wide[:HEAD, :BLK], wide[HEAD:, BLK:]], axis=0)


def virtual_pick(count, virtual_rows, pad_rows, part):
    shape = (count * virtual_rows, count * pad_rows)
    node = lax.broadcasted_iota(jnp.int32, shape, 0)
    place = lax.broadcasted_iota(jnp.int32, shape, 1)
    wanted = node // virtual_rows * pad_rows + part * virtual_rows + node % virtual_rows
    return (wanted == place).astype(jnp.bfloat16)


def relay_kernel(half, asked_ref, held_ref, pay_ref, pieces):
    count = held_ref.shape[0]
    own_blocks, piece = pieces.shape[0] // count, pieces.shape[1]
    start = pl.program_id(0) * pay_ref.shape[0]

    @pl.when(start == 0)
    def _():
        @pl.loop(0, count, unroll=4)
        def _(owner):
            found = held_ref[owner, pl.ds(0, own_blocks * piece), :].astype(jnp.float32)
            pieces[pl.ds(owner * own_blocks, own_blocks)] = found.reshape(own_blocks, piece, HALF)

    @pl.loop(0, pay_ref.shape[0], unroll=2)
    def _(device):
        for first in range(0, own_blocks * XG, 2):
            pair = [pieces[asked_ref[start + device, first + at]] for at in range(2)]
            pay_ref[device, pl.ds(first * piece, 2 * piece), :] = jnp.concatenate(
                pair, axis=0
            ).astype(jnp.bfloat16)


def relay(half, asked, held, own_blocks):
    count = held.shape[0]
    piece = PAIR // count
    return pl.pallas_call(
        functools.partial(relay_kernel, half),
        grid=(STEPS,),
        out_shape=jax.ShapeDtypeStruct((count, own_blocks * XG * piece, HALF), jnp.bfloat16),
        in_specs=[
            pl.BlockSpec(memory_space=pltpu.SMEM),
            pl.BlockSpec(held.shape[:2] + (HALF,), lambda i: (0, 0, half)),
        ],
        out_specs=pl.BlockSpec((count // STEPS, own_blocks * XG * piece, HALF), lambda i: (i, 0, 0)),
        scratch_shapes=[pltpu.VMEM((count * own_blocks, piece, HALF), jnp.float32)],
        compiler_params=pltpu.CompilerParams(vmem_limit_bytes=VMEM_LIMIT),
    )(asked, held)


def gather_kernel(asked_ref, back_ref, virtual_ref, out_ref, *partial):
    count, pad_rows = virtual_ref.shape[0], virtual_ref.shape[1]
    own_blocks, piece = partial[0].shape[0] // count, partial[0].shape[1]
    held = own_blocks * piece
    step = pl.program_id(0)

    @pl.when(step == 0)
    def _():
        for sums in partial:
            sums[...] = jnp.zeros_like(sums)

    @pl.loop(0, back_ref.shape[0], step=len(partial))
    def _(device):
        for first in range(0, own_blocks * XG, XG):
            for at, sums in enumerate(partial):
                terms = back_ref[device + at, pl.ds(first * piece, XG * piece), :].astype(jnp.float32)
                row = step * back_ref.shape[0] + device + at
                places = [asked_ref[row, first + j] for j in range(XG)]
                found = [sums[place] for place in places]
                for j, place in enumerate(places):
                    sums[place] = found[j] + terms[j * piece : (j + 1) * piece]

    @pl.when(step == pl.num_programs(0) - 1)
    def _():
        @pl.loop(0, count, unroll=4)
        def _(owner):
            span = pl.ds(owner * own_blocks, own_blocks)
            found = functools.reduce(lambda a, b: a + b, [sums[span] for sums in partial])
            out_ref[owner, pl.ds(0, held), :] = found.reshape(held, HALF).astype(jnp.bfloat16)
            out_ref[owner, pl.ds(held, pad_rows), :] = virtual_ref[owner]


def gather(half, asked, back, virtual, earlier):
    count, pad_rows = virtual.shape[0], virtual.shape[1]
    piece = PAIR // count
    own_blocks = back.shape[1] // (XG * piece)
    rows = own_blocks * piece + pad_rows

    def body(*refs):
        gather_kernel(*refs[:3], *refs[3 + len(earlier) :])

    return pl.pallas_call(
        body,
        grid=(STEPS,),
        out_shape=jax.ShapeDtypeStruct((count, rows, FEAT), jnp.bfloat16),
        in_specs=[
            pl.BlockSpec(memory_space=pltpu.SMEM),
            pl.BlockSpec((count // STEPS,) + back.shape[1:], lambda i: (i, 0, 0)),
            pl.BlockSpec(virtual.shape, lambda i: (0, 0, 0)),
        ]
        + [pl.BlockSpec(memory_space=pl.ANY)] * len(earlier),
        out_specs=pl.BlockSpec((count, rows, HALF), lambda i: (0, 0, half)),
        scratch_shapes=[pltpu.VMEM((count * own_blocks, piece, HALF), jnp.float32)] * 4,
        input_output_aliases={3 + i: i for i in range(len(earlier))},
        compiler_params=pltpu.CompilerParams(vmem_limit_bytes=VMEM_LIMIT),
    )(asked, back, virtual, *earlier)


def attend_kernel(
    sizes,
    half,
    chosen_ref,
    query_ref,
    grad_ref,
    own_ref,
    below_ref,
    above_ref,
    far_refs,
    held_ref,
    pay_ref,
    target_ref,
    query_grad_ref,
    below_out,
    above_out,
    far_outs,
    own_out,
    virtual_out,
    pay_out,
    table,
    flipped,
    tail,
    asked,
    total,
    scratch,
    sems,
):
    own_blocks, far_count, count, virtual_rows, pad_rows = sizes
    piece = PAIR // count
    far_start = own_blocks + 2 * HB
    virtual_at = far_start + far_count * own_blocks
    slots_at = virtual_at + 1
    step = pl.program_id(0)

    @pl.when(step == 0)
    def _():
        columns = pl.ds(half * HALF, HALF)
        moves = [
            (below_ref.at[:, :, columns], table.at[pl.ds(0, HB)]),
            (own_ref.at[:, :, columns], table.at[pl.ds(HB, own_blocks)]),
            (above_ref.at[:, :, columns], table.at[pl.ds(HB + own_blocks, HB)]),
        ]
        for k, far_ref in enumerate(far_refs):
            moves.append((far_ref.at[:, :, columns], table.at[pl.ds(far_start + k * own_blocks, own_blocks)]))
        moves.append((pay_ref, asked))
        moves.append((held_ref.at[:, pl.ds(own_blocks * piece, pad_rows), columns], tail))
        copies = [
            pltpu.make_async_copy(source, target, sems.at[i])
            for i, (source, target) in enumerate(moves)
        ]
        for copy in copies:
            copy.start()
        total[...] = jnp.zeros_like(total)
        copies[-1].wait()
        rows = tail[...].reshape(count * pad_rows, HALF)
        for part in range(2):
            pick = virtual_pick(count, virtual_rows, pad_rows, part)
            table[virtual_at, pl.ds(part * BLK, BLK), :] = dot(pick, rows).astype(jnp.bfloat16)

        for copy in copies[:-2]:
            copy.wait()

        @pl.loop(0, virtual_at + 1, unroll=7)
        def _(i):
            for part in range(2):
                rows = pl.ds(part * BLK, BLK)
                flipped[i, rows, :] = flip(table[i, rows, :])

        copies[-2].wait()

        @pl.loop(0, count, step=2)
        def _(device):
            rows = pl.ds(pl.multiple_of(device * piece, 2 * piece), 2 * piece)
            for first in range(0, own_blocks * XG, 2):
                span = pl.ds(first * piece, 2 * piece)
                pair = [asked[device + at, span, :].astype(jnp.float32) for at in range(2)]
                for at in range(2):
                    part = slice(at * piece, (at + 1) * piece)
                    table[slots_at + first + at, rows, :] = jnp.concatenate(
                        [pair[0][part], pair[1][part]], axis=0
                    ).astype(jnp.bfloat16)

    def work(sub):
        here = pl.ds(sub * BLK, BLK)
        block = step * BLOCKS_AT_ONCE + sub
        query = query_ref[here, :] * jnp.asarray(HEAD**-0.5, jnp.bfloat16)
        cotangent = grad_ref[here, :]
        cotangent_t = flip(cotangent)
        query_cols = heads_on_lanes(flip(query))
        query_rows = heads_on_rows(query)
        grad_cols = heads_on_lanes(cotangent_t)
        grad_rows = heads_on_rows(cotangent)

        listed = [chosen_ref[block, j] for j in range(LOC + XF)]
        listed += [slots_at + block * XG + j for j in range(XG)]
        groups = [listed[j : j + 4] for j in range(0, LOC + XF + XG, 4)] + [[virtual_at]]
        slot_group = len(groups) - 2
        K = pl.ds(0, BLK)
        V = pl.ds(BLK, BLK)

        def rows_of(group, part):
            return jnp.concatenate([table[i, part, :] for i in group], axis=0)

        def flipped_of(number, part):
            group = groups[number]
            if number == slot_group:
                return jnp.concatenate([flip(table[i, part, :]) for i in group], axis=1)
            return jnp.concatenate([flipped[i, part, :] for i in group], axis=1)

        def deposit(number, part, terms):
            if number != slot_group:
                for at, i in enumerate(groups[number]):
                    total[i, pl.ds(part * BLK, BLK), :] += terms[at * BLK : (at + 1) * BLK]
                return
            for first in range(0, XG, 2):
                start = (sub * XG + first) * piece
                for place in range(BLK // piece):
                    rows = [
                        terms[at * BLK + place * piece : at * BLK + (place + 1) * piece]
                        for at in (first, first + 1)
                    ]
                    pay_out[part * (BLK // piece) + place, pl.ds(start, 2 * piece), :] = (
                        jnp.concatenate(rows, axis=0).astype(jnp.bfloat16)
                    )

        spans, tops, sums = [], [], []
        start = 0
        for number, group in enumerate(groups):
            span = pl.ds(start, len(group) * BLK)
            start += len(group) * BLK
            scores = dot(rows_of(group, K), query_cols)
            top = jnp.max(scores, axis=0, keepdims=True)
            powers = jnp.exp(scores - top)
            scratch[sub, span, :] = powers
            spans.append(span)
            tops.append(top)
            sums.append(jnp.sum(powers, axis=0, keepdims=True))
            yield
        peak = functools.reduce(jnp.maximum, tops)
        factors = [jnp.exp(top - peak) for top in tops]
        norm = 1.0 / functools.reduce(lambda a, b: a + b, [f * s for f, s in zip(factors, sums)])
        factors = [f * norm for f in factors]

        target_wide = jnp.zeros((HALF, 2 * BLK), jnp.float32)
        for number, group in enumerate(groups):
            low = (scratch[sub, spans[number], :] * factors[number]).astype(jnp.bfloat16)
            target_wide += dot(flipped_of(number, V), low)
            deposit(number, 1, dot(low, grad_rows))
            yield
        target = own_head(target_wide).astype(jnp.bfloat16)
        target_ref[here, :] = flip(target)
        product = cotangent_t.astype(jnp.float32) * target.astype(jnp.float32)
        row_dot = jnp.concatenate(
            [
                jnp.sum(product[:HEAD], axis=0, keepdims=True),
                jnp.sum(product[HEAD:], axis=0, keepdims=True),
            ],
            axis=1,
        )

        query_wide = jnp.zeros((HALF, 2 * BLK), jnp.float32)
        for number, group in enumerate(groups):
            weights = scratch[sub, spans[number], :] * factors[number]
            grad_weights = dot(rows_of(group, V), grad_cols)
            grad_scores = (weights * (grad_weights - row_dot)).astype(jnp.bfloat16)
            query_wide += dot(flipped_of(number, K), grad_scores)
            deposit(number, 0, dot(grad_scores, query_rows))
            yield
        query_grad_ref[here, :] = own_head(query_wide).T * (HEAD**-0.5)
        yield

    groups_in_all = (LOC + XF + XG) // 4 + 1
    runs = [work(sub) for sub in range(BLOCKS_AT_ONCE)]
    for beat in range((2 + BLOCKS_AT_ONCE) * groups_in_all + 1):
        for sub, run in enumerate(runs):
            if beat >= sub * groups_in_all:
                next(run, None)

    @pl.when(step == pl.num_programs(0) - 1)
    def _():
        below_out[...] = total[pl.ds(0, HB)].astype(jnp.bfloat16)
        own_out[...] = total[pl.ds(HB, own_blocks)]
        above_out[...] = total[pl.ds(HB + own_blocks, HB)].astype(jnp.bfloat16)
        for k, far_out in enumerate(far_outs):
            far_out[...] = total[pl.ds(far_start + k * own_blocks, own_blocks)].astype(
                jnp.bfloat16
            )
        rows = jnp.zeros((count * pad_rows, HALF), jnp.float32)
        for part in range(2):
            pick = virtual_pick(count, virtual_rows, pad_rows, part)
            low = total[virtual_at, pl.ds(part * BLK, BLK), :].astype(jnp.bfloat16)
            rows += lax.dot_general(
                pick, low, (((0,), (0,)), ((), ())), preferred_element_type=jnp.float32
            )
        virtual_out[...] = rows.astype(jnp.bfloat16).reshape(count, pad_rows, HALF)


def attend(half, sizes, chosen, node_query, cotangent, own, near, held, pay, earlier):
    own_blocks, far_count, count, virtual_rows, pad_rows = sizes
    piece = PAIR // count
    rows = node_query.shape[0]
    kept = own_blocks + 2 * HB + far_count * own_blocks + 1
    listed = LOC + XF + XG
    column = pl.BlockSpec((BLOCKS_AT_ONCE * BLK, HALF), lambda i: (i, half))
    anywhere = pl.BlockSpec(memory_space=pl.ANY)
    block_shape = (own_blocks, PAIR, HALF)
    virtual_shape = (count, pad_rows, HALF)
    wide = pl.BlockSpec(block_shape, lambda i: (0, 0, half))

    def whole(shape):
        return pl.BlockSpec(shape, lambda i: (0,) * len(shape))

    inputs = 6 + len(near)

    def body(*refs):
        refs = list(refs)
        given, refs = refs[:inputs], refs[inputs + len(earlier) :]
        outs, scratch = refs[: 5 + len(near)], refs[5 + len(near) :]
        attend_kernel(
            sizes,
            half,
            *given[:6],
            given[6:-2],
            *given[-2:],
            *outs[:4],
            outs[4:-3],
            *outs[-3:],
            *scratch,
        )

    results = pl.pallas_call(
        body,
        grid=(own_blocks // BLOCKS_AT_ONCE,),
        out_shape=[
            jax.ShapeDtypeStruct((rows, FEAT), jnp.bfloat16),
            jax.ShapeDtypeStruct((rows, FEAT), jnp.float32),
            *[jax.ShapeDtypeStruct(own.shape, jnp.bfloat16) for _ in near],
            jax.ShapeDtypeStruct(block_shape, jnp.float32),
            jax.ShapeDtypeStruct(virtual_shape, jnp.bfloat16),
            jax.ShapeDtypeStruct(pay.shape, jnp.bfloat16),
        ],
        in_specs=[pl.BlockSpec(memory_space=pltpu.SMEM), column, column]
        + [anywhere] * (3 + len(near) + len(earlier)),
        out_specs=[column, column]
        + [wide] * len(near)
        + [whole(block_shape), whole(virtual_shape)]
        + [pl.BlockSpec((count, BLOCKS_AT_ONCE * XG * piece, HALF), lambda i: (0, i, 0))],
        scratch_shapes=[
            pltpu.VMEM((kept + own_blocks * XG, PAIR, HALF), jnp.bfloat16),
            pltpu.VMEM((kept, PAIR, HALF), jnp.bfloat16),
            pltpu.VMEM((count, pad_rows, HALF), jnp.bfloat16),
            pltpu.VMEM(pay.shape, jnp.bfloat16),
            pltpu.VMEM((kept, PAIR, HALF), jnp.float32),
            pltpu.VMEM((BLOCKS_AT_ONCE, (listed + 1) * BLK, 2 * BLK), jnp.float32),
            pltpu.SemaphoreType.DMA((3 + len(near),)),
        ],
        input_output_aliases={inputs + i: i for i in range(len(earlier))},
        compiler_params=pltpu.CompilerParams(
            vmem_limit_bytes=VMEM_LIMIT, dimension_semantics=("arbitrary",)
        ),
        cost_estimate=pl.CostEstimate(
            flops=12 * rows * (listed + 1) * BLK * HALF * 2,
            bytes_accessed=20 * 1024 * 1024,
            transcendentals=rows * (listed + 1) * BLK * 2,
        ),
    )(chosen, node_query, cotangent, own, *near, held, pay, *earlier)
    return results[:-3], results[-3:]


def settle_kernel(sizes, sum_refs, back_ref, key_out, value_out, virtual_key_out, virtual_value_out, total):
    own_blocks, _, count, virtual_rows, pad_rows = sizes
    piece = PAIR // count
    for half, sum_ref in enumerate(sum_refs):
        columns = pl.ds(half * HALF, HALF)
        total[...] = sum_ref[...]

        @pl.loop(0, count)
        def _(device):
            rows = pl.ds(pl.multiple_of(device * piece, piece), piece)
            back = back_ref[device, pl.ds(0, own_blocks * piece), columns].astype(jnp.float32)
            for block in range(own_blocks):
                total[block, rows, :] += back[block * piece : (block + 1) * piece]

        sums = total[...]
        key_out[:, columns] = sums[:, :BLK].reshape(own_blocks * BLK, HALF)
        value_out[:, columns] = sums[:, BLK:].reshape(own_blocks * BLK, HALF)
    tail = back_ref[:, pl.ds(own_blocks * piece, pad_rows), :].astype(jnp.float32)
    tail = jnp.sum(tail, axis=0)
    virtual_key_out[...] = tail[:virtual_rows]
    virtual_value_out[...] = tail[virtual_rows : 2 * virtual_rows]


def settle(sizes, sums, back):
    own_blocks, _, _, virtual_rows, _ = sizes
    rows = own_blocks * BLK

    def body(*refs):
        settle_kernel(sizes, refs[: len(sums)], *refs[len(sums) :])

    return pl.pallas_call(
        body,
        out_shape=[
            jax.ShapeDtypeStruct((rows, FEAT), jnp.float32),
            jax.ShapeDtypeStruct((rows, FEAT), jnp.float32),
            jax.ShapeDtypeStruct((virtual_rows, FEAT), jnp.float32),
            jax.ShapeDtypeStruct((virtual_rows, FEAT), jnp.float32),
        ],
        in_specs=[pl.BlockSpec(memory_space=pltpu.VMEM)] * (len(sums) + 1),
        out_specs=[pl.BlockSpec(memory_space=pltpu.VMEM)] * 4,
        scratch_shapes=[pltpu.VMEM((own_blocks, PAIR, HALF), jnp.float32)],
        compiler_params=pltpu.CompilerParams(vmem_limit_bytes=VMEM_LIMIT),
    )(*sums, back)


def per_device(
    node_query,
    node_key,
    node_value,
    cotangent,
    virtual_key,
    virtual_value,
    local_blocks,
    expander_dev,
    expander_pos,
    far_group,
    far_pos,
):
    count = lax.axis_size("dev")
    dom_count = lax.axis_size("dom")
    member = lax.axis_index("dev")
    own_blocks = local_blocks.shape[0]
    group_blocks = count * own_blocks
    virtual_rows = virtual_key.shape[0]
    pad_rows = -(-(2 * virtual_rows + 1) // 16) * 16
    far_count = dom_count - 1
    piece = PAIR // count
    sizes = (own_blocks, far_count, count, virtual_rows, pad_rows)

    far_start = own_blocks + 2 * HB
    chosen = jnp.concatenate(
        [
            (local_blocks % group_blocks - member * own_blocks + HB) % group_blocks,
            far_start + (far_group - 1) * own_blocks + far_pos,
        ],
        axis=1,
    ).astype(jnp.int32)

    own = jnp.concatenate(
        [
            node_key.reshape(own_blocks, BLK, FEAT),
            node_value.reshape(own_blocks, BLK, FEAT),
        ],
        axis=1,
    )
    pieces = own.reshape(own_blocks, count, piece, FEAT).transpose(1, 0, 2, 3)
    numbers = (expander_dev * own_blocks + expander_pos).reshape(1, -1).astype(jnp.bfloat16)
    tail = jnp.concatenate(
        [
            virtual_key,
            virtual_value,
            jnp.pad(numbers, ((0, pad_rows - 2 * virtual_rows - 1), (0, FEAT - numbers.shape[1]))),
        ],
        axis=0,
    )
    spread = jnp.concatenate(
        [
            pieces.reshape(count, own_blocks * piece, FEAT),
            jnp.broadcast_to(tail[None], (count, pad_rows, FEAT)),
        ],
        axis=1,
    )
    held = lax.all_to_all(spread, "dev", split_axis=0, concat_axis=0, tiled=True)
    asked = held[:, own_blocks * piece + 2 * virtual_rows, : own_blocks * XG].astype(jnp.int32)
    near = [
        shifted(own, "dev", 1),
        shifted(own, "dev", -1),
        *[shifted(own, "dom", -k) for k in range(1, dom_count)],
    ]
    sent = [relay(half, asked, held, own_blocks) for half in range(2)]
    longest = 2 + far_count // 2
    sent[0], near[:longest], near[longest + 1 :] = lax.optimization_barrier(
        (sent[0], near[:longest], near[longest + 1 :])
    )
    pays = [lax.all_to_all(sent[0], "dev", split_axis=0, concat_axis=0, tiled=True)]
    near, second = lax.optimization_barrier((near, sent[1]))
    pays.append(lax.all_to_all(second, "dev", split_axis=0, concat_axis=0, tiled=True))

    results, gathered, own_sums = [], [], []
    for half, pay in enumerate(pays):
        results, (own_sum, virtual_sum, pay_sum) = attend(
            half, sizes, chosen, node_query, cotangent, own, near, held, pay, results
        )
        own_sums.append(own_sum)
        back = lax.all_to_all(pay_sum, "dev", split_axis=0, concat_axis=0, tiled=True)
        gathered = [gather(half, asked, back, virtual_sum, gathered)]

    returned = lax.all_to_all(gathered[0], "dev", split_axis=0, concat_axis=0, tiled=True)
    attended, query_grad, below_sum, above_sum, *far_sums = results
    near_back = [
        shifted(below_sum, "dev", -1),
        shifted(above_sum, "dev", 1),
        *[shifted(term, "dom", k + 1) for k, term in enumerate(far_sums)],
    ]
    sums = [
        own_sum
        + sum(term[:, :, half * HALF : (half + 1) * HALF].astype(jnp.float32) for term in near_back)
        for half, own_sum in enumerate(own_sums)
    ]
    return (attended, query_grad, *settle(sizes, sums, returned))


def solution(mesh):
    spec = P(("dom", "dev"), None)
    return jax.shard_map(
        per_device, mesh=mesh, in_specs=(spec,) * 11, out_specs=(spec,) * 6, check_vma=False
    )
```

```python
import functools

import jax
import jax.numpy as jnp
from jax import lax
from jax.experimental import pallas as pl
from jax.experimental.pallas import tpu as pltpu
from jax.sharding import PartitionSpec as P

HB = 8
XG = 4
XF = 4
LOC = 16
BLK = 128
HEAD = 64
FEAT = 256
HALF = 128
PAIR = 2 * BLK
BLOCKS_AT_ONCE = 2
STEPS = 4
VMEM_LIMIT = 56 * 1024 * 1024


def shifted(value, axis, steps):
    count = lax.axis_size(axis)
    return lax.ppermute(value, axis, [(i, (i + steps) % count) for i in range(count)])


def dot(a, b):
    return jnp.dot(a, b, preferred_element_type=jnp.float32)


def flip(tile):
    return tile.T


def heads_on_lanes(tile_t):
    row = lax.broadcasted_iota(jnp.int32, tile_t.shape, 0)
    zero = jnp.zeros_like(tile_t)
    return jnp.concatenate(
        [jnp.where(row < HEAD, tile_t, zero), jnp.where(row >= HEAD, tile_t, zero)], axis=1
    )


def heads_on_rows(tile):
    column = lax.broadcasted_iota(jnp.int32, tile.shape, 1)
    zero = jnp.zeros_like(tile)
    return jnp.concatenate(
        [jnp.where(column < HEAD, tile, zero), jnp.where(column >= HEAD, tile, zero)], axis=0
    )


def own_head(wide):
    return jnp.concatenate([wide[:HEAD, :BLK], wide[HEAD:, BLK:]], axis=0)


def virtual_pick(count, virtual_rows, pad_rows, part):
    shape = (count * virtual_rows, count * pad_rows)
    node = lax.broadcasted_iota(jnp.int32, shape, 0)
    place = lax.broadcasted_iota(jnp.int32, shape, 1)
    wanted = node // virtual_rows * pad_rows + part * virtual_rows + node % virtual_rows
    return (wanted == place).astype(jnp.bfloat16)


def relay_kernel(half, asked_ref, held_ref, pay_ref, pieces):
    count = held_ref.shape[0]
    own_blocks, piece = pieces.shape[0] // count, pieces.shape[1]
    start = pl.program_id(0) * pay_ref.shape[0]

    @pl.when(start == 0)
    def _():
        @pl.loop(0, count)
        def _(owner):
            found = held_ref[owner, pl.ds(0, own_blocks * piece), :].astype(jnp.float32)
            pieces[pl.ds(owner * own_blocks, own_blocks)] = found.reshape(own_blocks, piece, HALF)

    @pl.loop(0, pay_ref.shape[0])
    def _(device):
        for first in range(0, own_blocks * XG, 2):
            pair = [pieces[asked_ref[start + device, first + at]] for at in range(2)]
            pay_ref[device, pl.ds(first * piece, 2 * piece), :] = jnp.concatenate(
                pair, axis=0
            ).astype(jnp.bfloat16)


def relay(half, asked, held, own_blocks):
    count = held.shape[0]
    piece = PAIR // count
    return pl.pallas_call(
        functools.partial(relay_kernel, half),
        grid=(STEPS,),
        out_shape=jax.ShapeDtypeStruct((count, own_blocks * XG * piece, HALF), jnp.bfloat16),
        in_specs=[
            pl.BlockSpec(memory_space=pltpu.SMEM),
            pl.BlockSpec(held.shape[:2] + (HALF,), lambda i: (0, 0, half)),
        ],
        out_specs=pl.BlockSpec((count // STEPS, own_blocks * XG * piece, HALF), lambda i: (i, 0, 0)),
        scratch_shapes=[pltpu.VMEM((count * own_blocks, piece, HALF), jnp.float32)],
        compiler_params=pltpu.CompilerParams(vmem_limit_bytes=VMEM_LIMIT),
    )(asked, held)


def gather_kernel(asked_ref, back_ref, virtual_ref, out_ref, *partial):
    count, pad_rows = virtual_ref.shape[0], virtual_ref.shape[1]
    own_blocks, piece = partial[0].shape[0] // count, partial[0].shape[1]
    held = own_blocks * piece
    step = pl.program_id(0)

    @pl.when(step == 0)
    def _():
        for sums in partial:
            sums[...] = jnp.zeros_like(sums)

    @pl.loop(0, back_ref.shape[0], step=len(partial))
    def _(device):
        for first in range(0, own_blocks * XG, XG):
            for at, sums in enumerate(partial):
                terms = back_ref[device + at, pl.ds(first * piece, XG * piece), :].astype(jnp.float32)
                row = step * back_ref.shape[0] + device + at
                places = [asked_ref[row, first + j] for j in range(XG)]
                found = [sums[place] for place in places]
                for j, place in enumerate(places):
                    sums[place] = found[j] + terms[j * piece : (j + 1) * piece]

    @pl.when(step == pl.num_programs(0) - 1)
    def _():
        @pl.loop(0, count)
        def _(owner):
            span = pl.ds(owner * own_blocks, own_blocks)
            found = functools.reduce(lambda a, b: a + b, [sums[span] for sums in partial])
            out_ref[owner, pl.ds(0, held), :] = found.reshape(held, HALF).astype(jnp.bfloat16)
            out_ref[owner, pl.ds(held, pad_rows), :] = virtual_ref[owner]


def gather(half, asked, back, virtual, earlier):
    count, pad_rows = virtual.shape[0], virtual.shape[1]
    piece = PAIR // count
    own_blocks = back.shape[1] // (XG * piece)
    rows = own_blocks * piece + pad_rows

    def body(*refs):
        gather_kernel(*refs[:3], *refs[3 + len(earlier) :])

    return pl.pallas_call(
        body,
        grid=(STEPS,),
        out_shape=jax.ShapeDtypeStruct((count, rows, FEAT), jnp.bfloat16),
        in_specs=[
            pl.BlockSpec(memory_space=pltpu.SMEM),
            pl.BlockSpec((count // STEPS,) + back.shape[1:], lambda i: (i, 0, 0)),
            pl.BlockSpec(virtual.shape, lambda i: (0, 0, 0)),
        ]
        + [pl.BlockSpec(memory_space=pl.ANY)] * len(earlier),
        out_specs=pl.BlockSpec((count, rows, HALF), lambda i: (0, 0, half)),
        scratch_shapes=[pltpu.VMEM((count * own_blocks, piece, HALF), jnp.float32)] * 4,
        input_output_aliases={3 + i: i for i in range(len(earlier))},
        compiler_params=pltpu.CompilerParams(vmem_limit_bytes=VMEM_LIMIT),
    )(asked, back, virtual, *earlier)


def attend_kernel(
    sizes,
    half,
    chosen_ref,
    query_ref,
    grad_ref,
    own_ref,
    below_ref,
    above_ref,
    far_refs,
    held_ref,
    pay_ref,
    target_ref,
    query_grad_ref,
    below_out,
    above_out,
    far_outs,
    own_out,
    virtual_out,
    pay_out,
    table,
    flipped,
    tail,
    asked,
    total,
    scratch,
    sems,
):
    own_blocks, far_count, count, virtual_rows, pad_rows = sizes
    piece = PAIR // count
    far_start = own_blocks + 2 * HB
    virtual_at = far_start + far_count * own_blocks
    slots_at = virtual_at + 1
    step = pl.program_id(0)

    @pl.when(step == 0)
    def _():
        columns = pl.ds(half * HALF, HALF)
        moves = [
            (below_ref.at[:, :, columns], table.at[pl.ds(0, HB)]),
            (own_ref.at[:, :, columns], table.at[pl.ds(HB, own_blocks)]),
            (above_ref.at[:, :, columns], table.at[pl.ds(HB + own_blocks, HB)]),
        ]
        for k, far_ref in enumerate(far_refs):
            moves.append((far_ref.at[:, :, columns], table.at[pl.ds(far_start + k * own_blocks, own_blocks)]))
        moves.append((pay_ref, asked))
        moves.append((held_ref.at[:, pl.ds(own_blocks * piece, pad_rows), columns], tail))
        copies = [
            pltpu.make_async_copy(source, target, sems.at[i])
            for i, (source, target) in enumerate(moves)
        ]
        for copy in copies:
            copy.start()
        total[...] = jnp.zeros_like(total)
        copies[-1].wait()
        rows = tail[...].reshape(count * pad_rows, HALF)
        for part in range(2):
            pick = virtual_pick(count, virtual_rows, pad_rows, part)
            table[virtual_at, pl.ds(part * BLK, BLK), :] = dot(pick, rows).astype(jnp.bfloat16)

        for copy in copies[:-2]:
            copy.wait()

        @pl.loop(0, virtual_at + 1, unroll=7)
        def _(i):
            for part in range(2):
                rows = pl.ds(part * BLK, BLK)
                flipped[i, rows, :] = flip(table[i, rows, :])

        copies[-2].wait()

        @pl.loop(0, count, step=2)
        def _(device):
            rows = pl.ds(pl.multiple_of(device * piece, 2 * piece), 2 * piece)
            for first in range(0, own_blocks * XG, 2):
                span = pl.ds(first * piece, 2 * piece)
                pair = [asked[device + at, span, :].astype(jnp.float32) for at in range(2)]
                for at in range(2):
                    part = slice(at * piece, (at + 1) * piece)
                    table[slots_at + first + at, rows, :] = jnp.concatenate(
                        [pair[0][part], pair[1][part]], axis=0
                    ).astype(jnp.bfloat16)

    def work(sub):
        here = pl.ds(sub * BLK, BLK)
        block = step * BLOCKS_AT_ONCE + sub
        query = query_ref[here, :] * jnp.asarray(HEAD**-0.5, jnp.bfloat16)
        cotangent = grad_ref[here, :]
        cotangent_t = flip(cotangent)
        query_cols = heads_on_lanes(flip(query))
        query_rows = heads_on_rows(query)
        grad_cols = heads_on_lanes(cotangent_t)
        grad_rows = heads_on_rows(cotangent)

        listed = [chosen_ref[block, j] for j in range(LOC + XF)]
        listed += [slots_at + block * XG + j for j in range(XG)]
        groups = [listed[j : j + 4] for j in range(0, LOC + XF + XG, 4)] + [[virtual_at]]
        slot_group = len(groups) - 2
        K = pl.ds(0, BLK)
        V = pl.ds(BLK, BLK)

        def rows_of(group, part):
            return jnp.concatenate([table[i, part, :] for i in group], axis=0)

        def flipped_of(number, part):
            group = groups[number]
            if number == slot_group:
                return jnp.concatenate([flip(table[i, part, :]) for i in group], axis=1)
            return jnp.concatenate([flipped[i, part, :] for i in group], axis=1)

        def deposit(number, part, terms):
            if number != slot_group:
                for at, i in enumerate(groups[number]):
                    total[i, pl.ds(part * BLK, BLK), :] += terms[at * BLK : (at + 1) * BLK]
                return
            for first in range(0, XG, 2):
                start = (sub * XG + first) * piece
                for place in range(BLK // piece):
                    rows = [
                        terms[at * BLK + place * piece : at * BLK + (place + 1) * piece]
                        for at in (first, first + 1)
                    ]
                    pay_out[part * (BLK // piece) + place, pl.ds(start, 2 * piece), :] = (
                        jnp.concatenate(rows, axis=0).astype(jnp.bfloat16)
                    )

        spans, tops, sums = [], [], []
        start = 0
        for number, group in enumerate(groups):
            span = pl.ds(start, len(group) * BLK)
            start += len(group) * BLK
            scores = dot(rows_of(group, K), query_cols)
            top = jnp.max(scores, axis=0, keepdims=True)
            powers = jnp.exp(scores - top)
            scratch[sub, span, :] = powers
            spans.append(span)
            tops.append(top)
            sums.append(jnp.sum(powers, axis=0, keepdims=True))
            yield
        peak = functools.reduce(jnp.maximum, tops)
        factors = [jnp.exp(top - peak) for top in tops]
        norm = 1.0 / functools.reduce(lambda a, b: a + b, [f * s for f, s in zip(factors, sums)])
        factors = [f * norm for f in factors]

        target_wide = jnp.zeros((HALF, 2 * BLK), jnp.float32)
        for number, group in enumerate(groups):
            low = (scratch[sub, spans[number], :] * factors[number]).astype(jnp.bfloat16)
            target_wide += dot(flipped_of(number, V), low)
            deposit(number, 1, dot(low, grad_rows))
            yield
        target = own_head(target_wide).astype(jnp.bfloat16)
        target_ref[here, :] = flip(target)
        product = cotangent_t.astype(jnp.float32) * target.astype(jnp.float32)
        row_dot = jnp.concatenate(
            [
                jnp.sum(product[:HEAD], axis=0, keepdims=True),
                jnp.sum(product[HEAD:], axis=0, keepdims=True),
            ],
            axis=1,
        )

        query_wide = jnp.zeros((HALF, 2 * BLK), jnp.float32)
        for number, group in enumerate(groups):
            weights = scratch[sub, spans[number], :] * factors[number]
            grad_weights = dot(rows_of(group, V), grad_cols)
            grad_scores = (weights * (grad_weights - row_dot)).astype(jnp.bfloat16)
            query_wide += dot(flipped_of(number, K), grad_scores)
            deposit(number, 0, dot(grad_scores, query_rows))
            yield
        query_grad_ref[here, :] = own_head(query_wide).T * (HEAD**-0.5)
        yield

    groups_in_all = (LOC + XF + XG) // 4 + 1
    runs = [work(sub) for sub in range(BLOCKS_AT_ONCE)]
    for beat in range((2 + BLOCKS_AT_ONCE) * groups_in_all + 1):
        for sub, run in enumerate(runs):
            if beat >= sub * groups_in_all:
                next(run, None)

    @pl.when(step == pl.num_programs(0) - 1)
    def _():
        below_out[...] = total[pl.ds(0, HB)].astype(jnp.bfloat16)
        own_out[...] = total[pl.ds(HB, own_blocks)]
        above_out[...] = total[pl.ds(HB + own_blocks, HB)].astype(jnp.bfloat16)
        for k, far_out in enumerate(far_outs):
            far_out[...] = total[pl.ds(far_start + k * own_blocks, own_blocks)].astype(
                jnp.bfloat16
            )
        rows = jnp.zeros((count * pad_rows, HALF), jnp.float32)
        for part in range(2):
            pick = virtual_pick(count, virtual_rows, pad_rows, part)
            low = total[virtual_at, pl.ds(part * BLK, BLK), :].astype(jnp.bfloat16)
            rows += lax.dot_general(
                pick, low, (((0,), (0,)), ((), ())), preferred_element_type=jnp.float32
            )
        virtual_out[...] = rows.astype(jnp.bfloat16).reshape(count, pad_rows, HALF)


def attend(half, sizes, chosen, node_query, cotangent, own, near, held, pay, earlier):
    own_blocks, far_count, count, virtual_rows, pad_rows = sizes
    piece = PAIR // count
    rows = node_query.shape[0]
    kept = own_blocks + 2 * HB + far_count * own_blocks + 1
    listed = LOC + XF + XG
    column = pl.BlockSpec((BLOCKS_AT_ONCE * BLK, HALF), lambda i: (i, half))
    anywhere = pl.BlockSpec(memory_space=pl.ANY)
    block_shape = (own_blocks, PAIR, HALF)
    virtual_shape = (count, pad_rows, HALF)
    wide = pl.BlockSpec(block_shape, lambda i: (0, 0, half))

    def whole(shape):
        return pl.BlockSpec(shape, lambda i: (0,) * len(shape))

    inputs = 6 + len(near)

    def body(*refs):
        refs = list(refs)
        given, refs = refs[:inputs], refs[inputs + len(earlier) :]
        outs, scratch = refs[: 5 + len(near)], refs[5 + len(near) :]
        attend_kernel(
            sizes,
            half,
            *given[:6],
            given[6:-2],
            *given[-2:],
            *outs[:4],
            outs[4:-3],
            *outs[-3:],
            *scratch,
        )

    results = pl.pallas_call(
        body,
        grid=(own_blocks // BLOCKS_AT_ONCE,),
        out_shape=[
            jax.ShapeDtypeStruct((rows, FEAT), jnp.bfloat16),
            jax.ShapeDtypeStruct((rows, FEAT), jnp.float32),
            *[jax.ShapeDtypeStruct(own.shape, jnp.bfloat16) for _ in near],
            jax.ShapeDtypeStruct(block_shape, jnp.float32),
            jax.ShapeDtypeStruct(virtual_shape, jnp.bfloat16),
            jax.ShapeDtypeStruct(pay.shape, jnp.bfloat16),
        ],
        in_specs=[pl.BlockSpec(memory_space=pltpu.SMEM), column, column]
        + [anywhere] * (3 + len(near) + len(earlier)),
        out_specs=[column, column]
        + [wide] * len(near)
        + [whole(block_shape), whole(virtual_shape)]
        + [pl.BlockSpec((count, BLOCKS_AT_ONCE * XG * piece, HALF), lambda i: (0, i, 0))],
        scratch_shapes=[
            pltpu.VMEM((kept + own_blocks * XG, PAIR, HALF), jnp.bfloat16),
            pltpu.VMEM((kept, PAIR, HALF), jnp.bfloat16),
            pltpu.VMEM((count, pad_rows, HALF), jnp.bfloat16),
            pltpu.VMEM(pay.shape, jnp.bfloat16),
            pltpu.VMEM((kept, PAIR, HALF), jnp.float32),
            pltpu.VMEM((BLOCKS_AT_ONCE, (listed + 1) * BLK, 2 * BLK), jnp.float32),
            pltpu.SemaphoreType.DMA((3 + len(near),)),
        ],
        input_output_aliases={inputs + i: i for i in range(len(earlier))},
        compiler_params=pltpu.CompilerParams(
            vmem_limit_bytes=VMEM_LIMIT, dimension_semantics=("arbitrary",)
        ),
        cost_estimate=pl.CostEstimate(
            flops=12 * rows * (listed + 1) * BLK * HALF * 2,
            bytes_accessed=20 * 1024 * 1024,
            transcendentals=rows * (listed + 1) * BLK * 2,
        ),
    )(chosen, node_query, cotangent, own, *near, held, pay, *earlier)
    return results[:-3], results[-3:]


def settle_kernel(sizes, sum_refs, back_ref, key_out, value_out, virtual_key_out, virtual_value_out, total):
    own_blocks, _, count, virtual_rows, pad_rows = sizes
    piece = PAIR // count
    for half, sum_ref in enumerate(sum_refs):
        columns = pl.ds(half * HALF, HALF)
        total[...] = sum_ref[...]

        @pl.loop(0, count)
        def _(device):
            rows = pl.ds(pl.multiple_of(device * piece, piece), piece)
            back = back_ref[device, pl.ds(0, own_blocks * piece), columns].astype(jnp.float32)
            for block in range(own_blocks):
                total[block, rows, :] += back[block * piece : (block + 1) * piece]

        sums = total[...]
        key_out[:, columns] = sums[:, :BLK].reshape(own_blocks * BLK, HALF)
        value_out[:, columns] = sums[:, BLK:].reshape(own_blocks * BLK, HALF)
    tail = back_ref[:, pl.ds(own_blocks * piece, pad_rows), :].astype(jnp.float32)
    tail = jnp.sum(tail, axis=0)
    virtual_key_out[...] = tail[:virtual_rows]
    virtual_value_out[...] = tail[virtual_rows : 2 * virtual_rows]


def settle(sizes, sums, back):
    own_blocks, _, _, virtual_rows, _ = sizes
    rows = own_blocks * BLK

    def body(*refs):
        settle_kernel(sizes, refs[: len(sums)], *refs[len(sums) :])

    return pl.pallas_call(
        body,
        out_shape=[
            jax.ShapeDtypeStruct((rows, FEAT), jnp.float32),
            jax.ShapeDtypeStruct((rows, FEAT), jnp.float32),
            jax.ShapeDtypeStruct((virtual_rows, FEAT), jnp.float32),
            jax.ShapeDtypeStruct((virtual_rows, FEAT), jnp.float32),
        ],
        in_specs=[pl.BlockSpec(memory_space=pltpu.VMEM)] * (len(sums) + 1),
        out_specs=[pl.BlockSpec(memory_space=pltpu.VMEM)] * 4,
        scratch_shapes=[pltpu.VMEM((own_blocks, PAIR, HALF), jnp.float32)],
        compiler_params=pltpu.CompilerParams(vmem_limit_bytes=VMEM_LIMIT),
    )(*sums, back)


def per_device(
    node_query,
    node_key,
    node_value,
    cotangent,
    virtual_key,
    virtual_value,
    local_blocks,
    expander_dev,
    expander_pos,
    far_group,
    far_pos,
):
    count = lax.axis_size("dev")
    dom_count = lax.axis_size("dom")
    member = lax.axis_index("dev")
    own_blocks = local_blocks.shape[0]
    group_blocks = count * own_blocks
    virtual_rows = virtual_key.shape[0]
    pad_rows = -(-(2 * virtual_rows + 1) // 16) * 16
    far_count = dom_count - 1
    piece = PAIR // count
    sizes = (own_blocks, far_count, count, virtual_rows, pad_rows)

    far_start = own_blocks + 2 * HB
    chosen = jnp.concatenate(
        [
            (local_blocks % group_blocks - member * own_blocks + HB) % group_blocks,
            far_start + (far_group - 1) * own_blocks + far_pos,
        ],
        axis=1,
    ).astype(jnp.int32)

    own = jnp.concatenate(
        [
            node_key.reshape(own_blocks, BLK, FEAT),
            node_value.reshape(own_blocks, BLK, FEAT),
        ],
        axis=1,
    )
    pieces = own.reshape(own_blocks, count, piece, FEAT).transpose(1, 0, 2, 3)
    numbers = (expander_dev * own_blocks + expander_pos).reshape(1, -1).astype(jnp.bfloat16)
    tail = jnp.concatenate(
        [
            virtual_key,
            virtual_value,
            jnp.pad(numbers, ((0, pad_rows - 2 * virtual_rows - 1), (0, FEAT - numbers.shape[1]))),
        ],
        axis=0,
    )
    spread = jnp.concatenate(
        [
            pieces.reshape(count, own_blocks * piece, FEAT),
            jnp.broadcast_to(tail[None], (count, pad_rows, FEAT)),
        ],
        axis=1,
    )
    held = lax.all_to_all(spread, "dev", split_axis=0, concat_axis=0, tiled=True)
    asked = held[:, own_blocks * piece + 2 * virtual_rows, : own_blocks * XG].astype(jnp.int32)
    near = [
        shifted(own, "dev", 1),
        shifted(own, "dev", -1),
        *[shifted(own, "dom", -k) for k in range(1, dom_count)],
    ]
    sent = [relay(half, asked, held, own_blocks) for half in range(2)]
    longest = 2 + far_count // 2
    sent[0], near[:longest], near[longest + 1 :] = lax.optimization_barrier(
        (sent[0], near[:longest], near[longest + 1 :])
    )
    pays = [lax.all_to_all(sent[0], "dev", split_axis=0, concat_axis=0, tiled=True)]
    near, second = lax.optimization_barrier((near, sent[1]))
    pays.append(lax.all_to_all(second, "dev", split_axis=0, concat_axis=0, tiled=True))

    results, gathered, own_sums = [], [], []
    for half, pay in enumerate(pays):
        results, (own_sum, virtual_sum, pay_sum) = attend(
            half, sizes, chosen, node_query, cotangent, own, near, held, pay, results
        )
        own_sums.append(own_sum)
        back = lax.all_to_all(pay_sum, "dev", split_axis=0, concat_axis=0, tiled=True)
        gathered = [gather(half, asked, back, virtual_sum, gathered)]

    returned = lax.all_to_all(gathered[0], "dev", split_axis=0, concat_axis=0, tiled=True)
    attended, query_grad, below_sum, above_sum, *far_sums = results
    near_back = [
        shifted(below_sum, "dev", -1),
        shifted(above_sum, "dev", 1),
        *[shifted(term, "dom", k + 1) for k, term in enumerate(far_sums)],
    ]
    sums = [
        own_sum
        + sum(term[:, :, half * HALF : (half + 1) * HALF].astype(jnp.float32) for term in near_back)
        for half, own_sum in enumerate(own_sums)
    ]
    return (attended, query_grad, *settle(sizes, sums, returned))


def solution(mesh):
    spec = P(("dom", "dev"), None)
    return jax.shard_map(
        per_device, mesh=mesh, in_specs=(spec,) * 11, out_specs=(spec,) * 6, check_vma=False
    )
```

```python
import functools

import jax
import jax.numpy as jnp
from jax import lax
from jax.experimental import pallas as pl
from jax.experimental.pallas import tpu as pltpu
from jax.sharding import PartitionSpec as P

HB = 8
XG = 4
XF = 4
LOC = 16
BLK = 128
HEAD = 64
FEAT = 256
HALF = 128
PAIR = 2 * BLK
BLOCKS_AT_ONCE = 2
STEPS = 4
VMEM_LIMIT = 24 * 1024 * 1024
ATTEND_VMEM = 44 * 1024 * 1024


def shifted(value, axis, steps):
    count = lax.axis_size(axis)
    return lax.ppermute(value, axis, [(i, (i + steps) % count) for i in range(count)])


def dot(a, b):
    return jnp.dot(a, b, preferred_element_type=jnp.float32)


def flip(tile):
    return tile.T


def heads_on_lanes(tile_t):
    row = lax.broadcasted_iota(jnp.int32, tile_t.shape, 0)
    zero = jnp.zeros_like(tile_t)
    return jnp.concatenate(
        [jnp.where(row < HEAD, tile_t, zero), jnp.where(row >= HEAD, tile_t, zero)], axis=1
    )


def heads_on_rows(tile):
    column = lax.broadcasted_iota(jnp.int32, tile.shape, 1)
    zero = jnp.zeros_like(tile)
    return jnp.concatenate(
        [jnp.where(column < HEAD, tile, zero), jnp.where(column >= HEAD, tile, zero)], axis=0
    )


def own_head(wide):
    return jnp.concatenate([wide[:HEAD, :BLK], wide[HEAD:, BLK:]], axis=0)


def virtual_pick(count, virtual_rows, pad_rows, part):
    shape = (count * virtual_rows, count * pad_rows)
    node = lax.broadcasted_iota(jnp.int32, shape, 0)
    place = lax.broadcasted_iota(jnp.int32, shape, 1)
    wanted = node // virtual_rows * pad_rows + part * virtual_rows + node % virtual_rows
    return (wanted == place).astype(jnp.bfloat16)


def relay_kernel(half, asked_ref, held_ref, pay_ref, pieces):
    count = held_ref.shape[0]
    own_blocks, piece = pieces.shape[0] // count, pieces.shape[1]
    start = pl.program_id(0) * pay_ref.shape[0]

    @pl.when(start == 0)
    def _():
        @pl.loop(0, count)
        def _(owner):
            found = held_ref[owner, pl.ds(0, own_blocks * piece), :].astype(jnp.float32)
            pieces[pl.ds(owner * own_blocks, own_blocks)] = found.reshape(own_blocks, piece, HALF)

    @pl.loop(0, pay_ref.shape[0])
    def _(device):
        for first in range(0, own_blocks * XG, 2):
            pair = [pieces[asked_ref[start + device, first + at]] for at in range(2)]
            pay_ref[device, pl.ds(first * piece, 2 * piece), :] = jnp.concatenate(
                pair, axis=0
            ).astype(jnp.bfloat16)


def relay(half, asked, held, own_blocks):
    count = held.shape[0]
    piece = PAIR // count
    return pl.pallas_call(
        functools.partial(relay_kernel, half),
        grid=(STEPS,),
        out_shape=jax.ShapeDtypeStruct((count, own_blocks * XG * piece, HALF), jnp.bfloat16),
        in_specs=[
            pl.BlockSpec(memory_space=pltpu.SMEM),
            pl.BlockSpec(held.shape[:2] + (HALF,), lambda i: (0, 0, half)),
        ],
        out_specs=pl.BlockSpec((count // STEPS, own_blocks * XG * piece, HALF), lambda i: (i, 0, 0)),
        scratch_shapes=[pltpu.VMEM((count * own_blocks, piece, HALF), jnp.float32)],
        compiler_params=pltpu.CompilerParams(vmem_limit_bytes=VMEM_LIMIT),
    )(asked, held)


def gather_kernel(asked_ref, back_ref, virtual_ref, out_ref, *partial):
    count, pad_rows = virtual_ref.shape[0], virtual_ref.shape[1]
    own_blocks, piece = partial[0].shape[0] // count, partial[0].shape[1]
    held = own_blocks * piece
    step = pl.program_id(0)

    @pl.when(step == 0)
    def _():
        for sums in partial:
            sums[...] = jnp.zeros_like(sums)

    @pl.loop(0, back_ref.shape[0], step=len(partial))
    def _(device):
        for first in range(0, own_blocks * XG, XG):
            for at, sums in enumerate(partial):
                terms = back_ref[device + at, pl.ds(first * piece, XG * piece), :].astype(jnp.float32)
                row = step * back_ref.shape[0] + device + at
                places = [asked_ref[row, first + j] for j in range(XG)]
                found = [sums[place] for place in places]
                for j, place in enumerate(places):
                    sums[place] = found[j] + terms[j * piece : (j + 1) * piece]

    @pl.when(step == pl.num_programs(0) - 1)
    def _():
        @pl.loop(0, count)
        def _(owner):
            span = pl.ds(owner * own_blocks, own_blocks)
            found = functools.reduce(lambda a, b: a + b, [sums[span] for sums in partial])
            out_ref[owner, pl.ds(0, held), :] = found.reshape(held, HALF).astype(jnp.bfloat16)
            out_ref[owner, pl.ds(held, pad_rows), :] = virtual_ref[owner]


def gather(half, asked, back, virtual, earlier):
    count, pad_rows = virtual.shape[0], virtual.shape[1]
    piece = PAIR // count
    own_blocks = back.shape[1] // (XG * piece)
    rows = own_blocks * piece + pad_rows

    def body(*refs):
        gather_kernel(*refs[:3], *refs[3 + len(earlier) :])

    return pl.pallas_call(
        body,
        grid=(STEPS,),
        out_shape=jax.ShapeDtypeStruct((count, rows, FEAT), jnp.bfloat16),
        in_specs=[
            pl.BlockSpec(memory_space=pltpu.SMEM),
            pl.BlockSpec((count // STEPS,) + back.shape[1:], lambda i: (i, 0, 0)),
            pl.BlockSpec(virtual.shape, lambda i: (0, 0, 0)),
        ]
        + [pl.BlockSpec(memory_space=pl.ANY)] * len(earlier),
        out_specs=pl.BlockSpec((count, rows, HALF), lambda i: (0, 0, half)),
        scratch_shapes=[pltpu.VMEM((count * own_blocks, piece, HALF), jnp.float32)] * 4,
        input_output_aliases={3 + i: i for i in range(len(earlier))},
        compiler_params=pltpu.CompilerParams(vmem_limit_bytes=VMEM_LIMIT),
    )(asked, back, virtual, *earlier)


def attend_kernel(
    sizes,
    half,
    chosen_ref,
    query_ref,
    grad_ref,
    own_ref,
    below_ref,
    above_ref,
    far_refs,
    held_ref,
    pay_ref,
    target_ref,
    query_grad_ref,
    below_out,
    above_out,
    far_outs,
    own_out,
    virtual_out,
    pay_out,
    table,
    flipped,
    tail,
    asked,
    total,
    scratch,
    sems,
):
    own_blocks, far_count, count, virtual_rows, pad_rows = sizes
    piece = PAIR // count
    far_start = own_blocks + 2 * HB
    virtual_at = far_start + far_count * own_blocks
    slots_at = virtual_at + 1
    step = pl.program_id(0)

    @pl.when(step == 0)
    def _():
        columns = pl.ds(half * HALF, HALF)
        moves = [
            (below_ref.at[:, :, columns], table.at[pl.ds(0, HB)]),
            (own_ref.at[:, :, columns], table.at[pl.ds(HB, own_blocks)]),
            (above_ref.at[:, :, columns], table.at[pl.ds(HB + own_blocks, HB)]),
        ]
        for k, far_ref in enumerate(far_refs):
            moves.append((far_ref.at[:, :, columns], table.at[pl.ds(far_start + k * own_blocks, own_blocks)]))
        moves.append((pay_ref, asked))
        moves.append((held_ref.at[:, pl.ds(own_blocks * piece, pad_rows), columns], tail))
        copies = [
            pltpu.make_async_copy(source, target, sems.at[i])
            for i, (source, target) in enumerate(moves)
        ]
        for copy in copies:
            copy.start()
        total[...] = jnp.zeros_like(total)
        copies[-1].wait()
        rows = tail[...].reshape(count * pad_rows, HALF)
        for part in range(2):
            pick = virtual_pick(count, virtual_rows, pad_rows, part)
            table[virtual_at, pl.ds(part * BLK, BLK), :] = dot(pick, rows).astype(jnp.bfloat16)

        for copy in copies[:-2]:
            copy.wait()

        @pl.loop(0, virtual_at + 1, unroll=7)
        def _(i):
            for part in range(2):
                rows = pl.ds(part * BLK, BLK)
                flipped[i, rows, :] = flip(table[i, rows, :])

        copies[-2].wait()

        @pl.loop(0, count, step=2)
        def _(device):
            rows = pl.ds(pl.multiple_of(device * piece, 2 * piece), 2 * piece)
            for first in range(0, own_blocks * XG, 2):
                span = pl.ds(first * piece, 2 * piece)
                pair = [asked[device + at, span, :].astype(jnp.float32) for at in range(2)]
                for at in range(2):
                    part = slice(at * piece, (at + 1) * piece)
                    table[slots_at + first + at, rows, :] = jnp.concatenate(
                        [pair[0][part], pair[1][part]], axis=0
                    ).astype(jnp.bfloat16)

    def work(sub):
        here = pl.ds(sub * BLK, BLK)
        block = step * BLOCKS_AT_ONCE + sub
        query = query_ref[here, :] * jnp.asarray(HEAD**-0.5, jnp.bfloat16)
        cotangent = grad_ref[here, :]
        cotangent_t = flip(cotangent)
        query_cols = heads_on_lanes(flip(query))
        query_rows = heads_on_rows(query)
        grad_cols = heads_on_lanes(cotangent_t)
        grad_rows = heads_on_rows(cotangent)

        listed = [chosen_ref[block, j] for j in range(LOC + XF)]
        listed += [slots_at + block * XG + j for j in range(XG)]
        groups = [listed[j : j + 4] for j in range(0, LOC + XF + XG, 4)] + [[virtual_at]]
        slot_group = len(groups) - 2
        K = pl.ds(0, BLK)
        V = pl.ds(BLK, BLK)

        def rows_of(group, part):
            return jnp.concatenate([table[i, part, :] for i in group], axis=0)

        def flipped_of(number, part):
            group = groups[number]
            if number == slot_group:
                return jnp.concatenate([flip(table[i, part, :]) for i in group], axis=1)
            return jnp.concatenate([flipped[i, part, :] for i in group], axis=1)

        def deposit(number, part, terms):
            if number != slot_group:
                for at, i in enumerate(groups[number]):
                    total[i, pl.ds(part * BLK, BLK), :] += terms[at * BLK : (at + 1) * BLK]
                return
            for first in range(0, XG, 2):
                start = (sub * XG + first) * piece
                for place in range(BLK // piece):
                    rows = [
                        terms[at * BLK + place * piece : at * BLK + (place + 1) * piece]
                        for at in (first, first + 1)
                    ]
                    pay_out[part * (BLK // piece) + place, pl.ds(start, 2 * piece), :] = (
                        jnp.concatenate(rows, axis=0).astype(jnp.bfloat16)
                    )

        spans, tops, sums = [], [], []
        start = 0
        for number, group in enumerate(groups):
            span = pl.ds(start, len(group) * BLK)
            start += len(group) * BLK
            scores = dot(rows_of(group, K), query_cols)
            top = jnp.max(scores, axis=0, keepdims=True)
            powers = jnp.exp(scores - top)
            scratch[sub, span, :] = powers
            spans.append(span)
            tops.append(top)
            sums.append(jnp.sum(powers, axis=0, keepdims=True))
            yield
        peak = functools.reduce(jnp.maximum, tops)
        factors = [jnp.exp(top - peak) for top in tops]
        norm = 1.0 / functools.reduce(lambda a, b: a + b, [f * s for f, s in zip(factors, sums)])
        factors = [f * norm for f in factors]

        target_wide = jnp.zeros((HALF, 2 * BLK), jnp.float32)
        for number, group in enumerate(groups):
            low = (scratch[sub, spans[number], :] * factors[number]).astype(jnp.bfloat16)
            target_wide += dot(flipped_of(number, V), low)
            deposit(number, 1, dot(low, grad_rows))
            yield
        target = own_head(target_wide).astype(jnp.bfloat16)
        target_ref[here, :] = flip(target)
        product = cotangent_t.astype(jnp.float32) * target.astype(jnp.float32)
        row_dot = jnp.concatenate(
            [
                jnp.sum(product[:HEAD], axis=0, keepdims=True),
                jnp.sum(product[HEAD:], axis=0, keepdims=True),
            ],
            axis=1,
        )

        query_wide = jnp.zeros((HALF, 2 * BLK), jnp.float32)
        for number, group in enumerate(groups):
            weights = scratch[sub, spans[number], :] * factors[number]
            grad_weights = dot(rows_of(group, V), grad_cols)
            grad_scores = (weights * (grad_weights - row_dot)).astype(jnp.bfloat16)
            query_wide += dot(flipped_of(number, K), grad_scores)
            deposit(number, 0, dot(grad_scores, query_rows))
            yield
        query_grad_ref[here, :] = own_head(query_wide).T * (HEAD**-0.5)
        yield

    groups_in_all = (LOC + XF + XG) // 4 + 1
    runs = [work(sub) for sub in range(BLOCKS_AT_ONCE)]
    for beat in range((2 + BLOCKS_AT_ONCE) * groups_in_all + 1):
        for sub, run in enumerate(runs):
            if beat >= sub * groups_in_all:
                next(run, None)

    @pl.when(step == pl.num_programs(0) - 1)
    def _():
        below_out[...] = total[pl.ds(0, HB)].astype(jnp.bfloat16)
        own_out[...] = total[pl.ds(HB, own_blocks)]
        above_out[...] = total[pl.ds(HB + own_blocks, HB)].astype(jnp.bfloat16)
        for k, far_out in enumerate(far_outs):
            far_out[...] = total[pl.ds(far_start + k * own_blocks, own_blocks)].astype(
                jnp.bfloat16
            )
        rows = jnp.zeros((count * pad_rows, HALF), jnp.float32)
        for part in range(2):
            pick = virtual_pick(count, virtual_rows, pad_rows, part)
            low = total[virtual_at, pl.ds(part * BLK, BLK), :].astype(jnp.bfloat16)
            rows += lax.dot_general(
                pick, low, (((0,), (0,)), ((), ())), preferred_element_type=jnp.float32
            )
        virtual_out[...] = rows.astype(jnp.bfloat16).reshape(count, pad_rows, HALF)


def attend(half, sizes, chosen, node_query, cotangent, own, near, held, pay, earlier):
    own_blocks, far_count, count, virtual_rows, pad_rows = sizes
    piece = PAIR // count
    rows = node_query.shape[0]
    kept = own_blocks + 2 * HB + far_count * own_blocks + 1
    listed = LOC + XF + XG
    column = pl.BlockSpec((BLOCKS_AT_ONCE * BLK, HALF), lambda i: (i, half))
    anywhere = pl.BlockSpec(memory_space=pl.ANY)
    block_shape = (own_blocks, PAIR, HALF)
    virtual_shape = (count, pad_rows, HALF)
    wide = pl.BlockSpec(block_shape, lambda i: (0, 0, half))

    def whole(shape):
        return pl.BlockSpec(shape, lambda i: (0,) * len(shape))

    inputs = 6 + len(near)

    def body(*refs):
        refs = list(refs)
        given, refs = refs[:inputs], refs[inputs + len(earlier) :]
        outs, scratch = refs[: 5 + len(near)], refs[5 + len(near) :]
        attend_kernel(
            sizes,
            half,
            *given[:6],
            given[6:-2],
            *given[-2:],
            *outs[:4],
            outs[4:-3],
            *outs[-3:],
            *scratch,
        )

    results = pl.pallas_call(
        body,
        grid=(own_blocks // BLOCKS_AT_ONCE,),
        out_shape=[
            jax.ShapeDtypeStruct((rows, FEAT), jnp.bfloat16),
            jax.ShapeDtypeStruct((rows, FEAT), jnp.float32),
            *[jax.ShapeDtypeStruct(own.shape, jnp.bfloat16) for _ in near],
            jax.ShapeDtypeStruct(block_shape, jnp.float32),
            jax.ShapeDtypeStruct(virtual_shape, jnp.bfloat16),
            jax.ShapeDtypeStruct(pay.shape, jnp.bfloat16),
        ],
        in_specs=[pl.BlockSpec(memory_space=pltpu.SMEM), column, column]
        + [anywhere] * (3 + len(near) + len(earlier)),
        out_specs=[column, column]
        + [wide] * len(near)
        + [whole(block_shape), whole(virtual_shape)]
        + [pl.BlockSpec((count, BLOCKS_AT_ONCE * XG * piece, HALF), lambda i: (0, i, 0))],
        scratch_shapes=[
            pltpu.VMEM((kept + own_blocks * XG, PAIR, HALF), jnp.bfloat16),
            pltpu.VMEM((kept, PAIR, HALF), jnp.bfloat16),
            pltpu.VMEM((count, pad_rows, HALF), jnp.bfloat16),
            pltpu.VMEM(pay.shape, jnp.bfloat16),
            pltpu.VMEM((kept, PAIR, HALF), jnp.float32),
            pltpu.VMEM((BLOCKS_AT_ONCE, (listed + 1) * BLK, 2 * BLK), jnp.float32),
            pltpu.SemaphoreType.DMA((3 + len(near),)),
        ],
        input_output_aliases={inputs + i: i for i in range(len(earlier))},
        compiler_params=pltpu.CompilerParams(
            vmem_limit_bytes=ATTEND_VMEM, dimension_semantics=("arbitrary",)
        ),
        cost_estimate=pl.CostEstimate(
            flops=12 * rows * (listed + 1) * BLK * HALF * 2,
            bytes_accessed=20 * 1024 * 1024,
            transcendentals=rows * (listed + 1) * BLK * 2,
        ),
    )(chosen, node_query, cotangent, own, *near, held, pay, *earlier)
    return results[:-3], results[-3:]


def settle_kernel(sizes, sum_refs, back_ref, key_out, value_out, virtual_key_out, virtual_value_out, total):
    own_blocks, _, count, virtual_rows, pad_rows = sizes
    piece = PAIR // count
    for half, sum_ref in enumerate(sum_refs):
        columns = pl.ds(half * HALF, HALF)
        total[...] = sum_ref[...]

        @pl.loop(0, count)
        def _(device):
            rows = pl.ds(pl.multiple_of(device * piece, piece), piece)
            back = back_ref[device, pl.ds(0, own_blocks * piece), columns].astype(jnp.float32)
            for block in range(own_blocks):
                total[block, rows, :] += back[block * piece : (block + 1) * piece]

        sums = total[...]
        key_out[:, columns] = sums[:, :BLK].reshape(own_blocks * BLK, HALF)
        value_out[:, columns] = sums[:, BLK:].reshape(own_blocks * BLK, HALF)
    tail = back_ref[:, pl.ds(own_blocks * piece, pad_rows), :].astype(jnp.float32)
    tail = jnp.sum(tail, axis=0)
    virtual_key_out[...] = tail[:virtual_rows]
    virtual_value_out[...] = tail[virtual_rows : 2 * virtual_rows]


def settle(sizes, sums, back):
    own_blocks, _, _, virtual_rows, _ = sizes
    rows = own_blocks * BLK

    def body(*refs):
        settle_kernel(sizes, refs[: len(sums)], *refs[len(sums) :])

    return pl.pallas_call(
        body,
        out_shape=[
            jax.ShapeDtypeStruct((rows, FEAT), jnp.float32),
            jax.ShapeDtypeStruct((rows, FEAT), jnp.float32),
            jax.ShapeDtypeStruct((virtual_rows, FEAT), jnp.float32),
            jax.ShapeDtypeStruct((virtual_rows, FEAT), jnp.float32),
        ],
        in_specs=[pl.BlockSpec(memory_space=pltpu.VMEM)] * (len(sums) + 1),
        out_specs=[pl.BlockSpec(memory_space=pltpu.VMEM)] * 4,
        scratch_shapes=[pltpu.VMEM((own_blocks, PAIR, HALF), jnp.float32)],
        compiler_params=pltpu.CompilerParams(vmem_limit_bytes=VMEM_LIMIT),
    )(*sums, back)


def per_device(
    node_query,
    node_key,
    node_value,
    cotangent,
    virtual_key,
    virtual_value,
    local_blocks,
    expander_dev,
    expander_pos,
    far_group,
    far_pos,
):
    count = lax.axis_size("dev")
    dom_count = lax.axis_size("dom")
    member = lax.axis_index("dev")
    own_blocks = local_blocks.shape[0]
    group_blocks = count * own_blocks
    virtual_rows = virtual_key.shape[0]
    pad_rows = -(-(2 * virtual_rows + 1) // 16) * 16
    far_count = dom_count - 1
    piece = PAIR // count
    sizes = (own_blocks, far_count, count, virtual_rows, pad_rows)

    far_start = own_blocks + 2 * HB
    chosen = jnp.concatenate(
        [
            (local_blocks % group_blocks - member * own_blocks + HB) % group_blocks,
            far_start + (far_group - 1) * own_blocks + far_pos,
        ],
        axis=1,
    ).astype(jnp.int32)

    own = jnp.concatenate(
        [
            node_key.reshape(own_blocks, BLK, FEAT),
            node_value.reshape(own_blocks, BLK, FEAT),
        ],
        axis=1,
    )
    pieces = own.reshape(own_blocks, count, piece, FEAT).transpose(1, 0, 2, 3)
    numbers = (expander_dev * own_blocks + expander_pos).reshape(1, -1).astype(jnp.bfloat16)
    tail = jnp.concatenate(
        [
            virtual_key,
            virtual_value,
            jnp.pad(numbers, ((0, pad_rows - 2 * virtual_rows - 1), (0, FEAT - numbers.shape[1]))),
        ],
        axis=0,
    )
    spread = jnp.concatenate(
        [
            pieces.reshape(count, own_blocks * piece, FEAT),
            jnp.broadcast_to(tail[None], (count, pad_rows, FEAT)),
        ],
        axis=1,
    )
    held = lax.all_to_all(spread, "dev", split_axis=0, concat_axis=0, tiled=True)
    asked = held[:, own_blocks * piece + 2 * virtual_rows, : own_blocks * XG].astype(jnp.int32)
    near = [
        shifted(own, "dev", 1),
        shifted(own, "dev", -1),
        *[shifted(own, "dom", -k) for k in range(1, dom_count)],
    ]
    sent = [relay(half, asked, held, own_blocks) for half in range(2)]
    longest = 2 + far_count // 2
    sent[0], near[:longest], near[longest + 1 :] = lax.optimization_barrier(
        (sent[0], near[:longest], near[longest + 1 :])
    )
    pays = [lax.all_to_all(sent[0], "dev", split_axis=0, concat_axis=0, tiled=True)]
    near, second = lax.optimization_barrier((near, sent[1]))
    pays.append(lax.all_to_all(second, "dev", split_axis=0, concat_axis=0, tiled=True))

    results, gathered, own_sums = [], [], []
    for half, pay in enumerate(pays):
        results, (own_sum, virtual_sum, pay_sum) = attend(
            half, sizes, chosen, node_query, cotangent, own, near, held, pay, results
        )
        own_sums.append(own_sum)
        back = lax.all_to_all(pay_sum, "dev", split_axis=0, concat_axis=0, tiled=True)
        gathered = [gather(half, asked, back, virtual_sum, gathered)]

    returned = lax.all_to_all(gathered[0], "dev", split_axis=0, concat_axis=0, tiled=True)
    attended, query_grad, below_sum, above_sum, *far_sums = results
    near_back = [
        shifted(below_sum, "dev", -1),
        shifted(above_sum, "dev", 1),
        *[shifted(term, "dom", k + 1) for k, term in enumerate(far_sums)],
    ]
    sums = [
        own_sum
        + sum(term[:, :, half * HALF : (half + 1) * HALF].astype(jnp.float32) for term in near_back)
        for half, own_sum in enumerate(own_sums)
    ]
    return (attended, query_grad, *settle(sizes, sums, returned))


def solution(mesh):
    spec = P(("dom", "dev"), None)
    return jax.shard_map(
        per_device, mesh=mesh, in_specs=(spec,) * 11, out_specs=(spec,) * 6, check_vma=False
    )
```
